32 devices in a mesh: node: 2 (over x), row: 16 (over z, y, core).
Axes of the slice: x: 2, y: 2, z: 4, core: 2. Of those that a mesh axis runs over, the one named last changes fastest.
Arguments:
- leaves: float32 [4, 8192, 256], P('node', 'row'), may hold values from -200 to 200
- level_one: float32 [2, 256, 256, 256], P('node', 'row'), may hold values from -20 to 20
- level_two: float32 [2, 128, 256, 256], P('node', 'row'), may hold values from -20 to 20
Outputs:
- leaf_bases: float32 [4, 8192, 256], P('node', 'row')
- level_one_bases: float32 [2, 256, 256, 256], P('node', None, 'row')
- level_two_bases: float32 [2, 128, 256, 256], P('node', None, 'row')
- level_two_factors: float32 [2, 256, 256], P('node')
The draws below stay inside these ranges and needn't reach their ends.
All inputs are finite; a program needn't handle non-finite values.
Results may differ from the reference program's by a relative error of at most 0.0003.
Values sent between devices are 32-bit elements; how exact they have to be, the bound alone decides.
No kernel may reach another device: no remote copies, remote signals or barrier semaphores. Data moves between devices by JAX's collectives and lax.ppermute only.
A program may use at most 64 MiB of HBM per device.

```python
import math
import jax
import jax.numpy as jnp
from jax import lax

R = 256
LEAF_ROWS = 8192
LEAVES = 4
N_NODE = 2


def column_mixed(base_draw):
    return base_draw + 0.6 * jnp.roll(base_draw, 1, axis=-1)


def scaled_tensor(key_list, base_draw):
    full_shape = base_draw.shape
    scale_shape = (full_shape[0], 1, 1, full_shape[3])
    col_scale = jnp.exp(jax.random.uniform(key_list[1], scale_shape, jnp.float32, math.log(0.3), math.log(3.0)))
    return column_mixed(base_draw) * col_scale


def draw_leaves(key, part):
    key_list = jax.random.split(jax.random.fold_in(key, 101), 3)
    full_shape = (LEAVES, LEAF_ROWS, R)
    base_draw = jnp.clip(jax.random.normal(key_list[0], full_shape, jnp.float32), -4.0, 4.0)
    mixed = column_mixed(base_draw)
    row_ramp = jnp.arange(LEAF_ROWS, dtype=jnp.float32)[None, :, None] * (math.log(3.0) / LEAF_ROWS)
    row_scale = jnp.exp(jax.random.uniform(key_list[1], (LEAVES, LEAF_ROWS, 1), jnp.float32, -1.15, 1.15) + row_ramp)
    col_scale = jnp.exp(jax.random.uniform(key_list[2], (LEAVES, 1, R), jnp.float32, math.log(0.3), math.log(3.0)))
    values = mixed * row_scale * col_scale
    return values


def draw_level_one(key, part):
    key_list = jax.random.split(jax.random.fold_in(key, 202), 2)
    full_shape = (LEAVES // 2, R, R, R)
    base_draw = jnp.clip(jax.random.normal(key_list[0], full_shape, jnp.float32), -4.0, 4.0)
    return scaled_tensor(key_list, base_draw)


def draw_level_two(key, part):
    key_list = jax.random.split(jax.random.fold_in(key, 303), 2)
    full_shape = (LEAVES // 2, R // 2, R, R)
    base_draw = jnp.clip(jax.random.normal(key_list[0], full_shape, jnp.float32), -4.0, 4.0)
    return scaled_tensor(key_list, base_draw)


def setup_inputs(seed: int = 0) -> dict:
    keys = jax.random.split(jax.random.key(seed), 4)
    return {
        "leaves": draw_leaves(jax.random.fold_in(keys[3], 71), 0),
        "level_one": draw_level_one(jax.random.fold_in(keys[3], 71), 0),
        "level_two": draw_level_two(jax.random.fold_in(keys[3], 71), 0),
    }


PRECISE = lax.Precision.HIGHEST

def factored(gram_matrix):
    width = gram_matrix.shape[-1]
    lower = jnp.linalg.cholesky(gram_matrix)
    identity = jnp.eye(width, dtype=gram_matrix.dtype)
    inverse_lower = jax.scipy.linalg.solve_triangular(lower, identity, lower=True)
    return (lower.T, inverse_lower.T)

def leaf_step(leaf_basis):
    gram_matrix = jnp.dot(leaf_basis.T.astype(jnp.float32), leaf_basis.astype(jnp.float32), precision=PRECISE, preferred_element_type=jnp.float32) / LEAF_ROWS
    upper_factor, inverse = factored(gram_matrix)
    new_bases = jnp.dot(leaf_basis.astype(jnp.float32), inverse.astype(jnp.float32), precision=PRECISE, preferred_element_type=jnp.float32)
    return (new_bases, upper_factor)

def tensor_step(operands):
    tensor, left_factor, right_factor = operands
    moved_one = jnp.einsum('ia,abk->ibk', left_factor, tensor, precision=PRECISE)
    moved_one = jnp.einsum('jb,ibk->ijk', right_factor, moved_one, precision=PRECISE)
    flat_rows = moved_one.reshape(R * R, R)
    gram_matrix = jnp.dot(flat_rows.T.astype(jnp.float32), flat_rows.astype(jnp.float32), precision=PRECISE, preferred_element_type=jnp.float32) / (R * R)
    upper_factor, inverse = factored(gram_matrix)
    new_bases = jnp.dot(flat_rows.astype(jnp.float32), inverse.astype(jnp.float32), precision=PRECISE, preferred_element_type=jnp.float32).reshape(R, R, R)
    return (new_bases, upper_factor)

def reference(leaves, level_one, level_two):
    leaf_bases, leaf_factors = lax.map(leaf_step, leaves)
    level_one_bases, one_factors = lax.map(tensor_step, (level_one, leaf_factors[0::2], leaf_factors[1::2]))
    pair_count = N_NODE // 2
    natural = level_two.reshape(pair_count, 2, R // 2, R, R).transpose(0, 2, 1, 3, 4).reshape(pair_count, R, R, R)
    two_bases, two_factors = lax.map(tensor_step, (natural, one_factors[0::2], one_factors[1::2]))
    level_two_bases = two_bases.reshape(pair_count, R // 2, 2, R, R).transpose(0, 2, 1, 3, 4).reshape(N_NODE, R // 2, R, R)
    level_two_factors = jnp.repeat(two_factors, 2, axis=0)
    return (leaf_bases, level_one_bases, level_two_bases, level_two_factors)
```

```python
import functools
import jax
import jax.numpy as jnp
from jax import lax
from jax.experimental import pallas as pl
from jax.experimental.pallas import tpu as pltpu
from jax.sharding import PartitionSpec as P

PRECISE = lax.Precision.HIGHEST
FAST = lax.Precision.HIGH
SUB = 8
LANE = 128


def swapped(value, axis, mask):
    pairs = [(source, source ^ mask) for source in range(lax.axis_size(axis))]
    return lax.ppermute(value, axis, pairs)


def pick(value, index):
    return lax.dynamic_index_in_dim(value, index, 0, keepdims=False)


def factor_kernel(scale, gram_ref, upper_ref, inverse_ref, work_ref):
    n = gram_ref.shape[0]
    work_ref[:, :n] = gram_ref[...] * scale
    row_ids = lax.broadcasted_iota(jnp.int32, (n, n), 0)
    col_ids = lax.broadcasted_iota(jnp.int32, (n, n), 1)
    work_ref[:, n:] = jnp.where(row_ids == col_ids, 1.0, 0.0)
    for start in range(0, n, SUB):
        first = (start // LANE) * LANE
        end = n + ((start + SUB + LANE - 1) // LANE) * LANE
        width = end - first
        offset = start - first
        panel = work_ref[start : start + SUB, first:end]
        rows = [jnp.broadcast_to(panel[i : i + 1, :], (SUB, width)) for i in range(SUB)]
        diag = {}
        for i in range(SUB):
            for j in range(i, SUB):
                entry = rows[i][:, offset + j : offset + j + 1]
                diag[i, j] = jnp.broadcast_to(entry, (SUB, LANE))
        sub_ids = lax.broadcasted_iota(jnp.int32, (SUB, width), 0)
        done = jnp.zeros((SUB, width), jnp.float32)
        for i in range(SUB):
            root = lax.rsqrt(diag[i, i])
            row = rows[i] * jnp.concatenate([root] * (width // LANE), axis=1)
            done = jnp.where(sub_ids == i, row, done)
            coef = {j: diag[i, j] * root for j in range(i + 1, SUB)}
            for j in range(i + 1, SUB):
                for l in range(j, SUB):
                    diag[j, l] = diag[j, l] - coef[j] * coef[l]
                rows[j] = rows[j] - jnp.concatenate([coef[j]] * (width // LANE), axis=1) * row
        lane_ids = lax.broadcasted_iota(jnp.int32, (SUB, width), 1)
        done = jnp.where(lane_ids >= offset + sub_ids, done, 0.0)
        if first:
            upper_ref[start : start + SUB, :first] = jnp.zeros((SUB, first), jnp.float32)
        upper_ref[start : start + SUB, first:] = done[:, : n - first]
        inverse_ref[start : start + SUB, : end - n] = done[:, n - first :]
        if end < 2 * n:
            inverse_ref[start : start + SUB, end - n :] = jnp.zeros((SUB, 2 * n - end), jnp.float32)
        below = start + SUB
        if below < n:
            left = (below // LANE) * LANE
            product = lax.dot_general(
                done[:, left - first : n - first],
                done[:, left - first :],
                (((0,), (0,)), ((), ())),
                precision=PRECISE,
                preferred_element_type=jnp.float32,
            )
            work_ref[below:, left:end] = work_ref[below:, left:end] - product[below - left :, :]


def factored(gram_matrix, scale):
    n = gram_matrix.shape[0]
    square = jax.ShapeDtypeStruct((n, n), jnp.float32)
    return pl.pallas_call(
        functools.partial(factor_kernel, scale),
        out_shape=(square, square),
        in_specs=[pl.BlockSpec(memory_space=pltpu.VMEM)],
        out_specs=(pl.BlockSpec(memory_space=pltpu.VMEM),) * 2,
        scratch_shapes=[pltpu.VMEM((n, 2 * n), jnp.float32)],
        compiler_params=pltpu.CompilerParams(vmem_limit_bytes=32 * 2**20),
        name="factor",
    )(gram_matrix)


def groups_of(size):
    return [list(range(0, size, 2)), list(range(1, size, 2))]


def scattered(value):
    size = lax.axis_size("row")
    core = lax.axis_index("row") % 2
    kept = pick(value, core) + swapped(pick(value, 1 - core), "row", 1)
    moved = lax.all_to_all(
        kept, "row", 0, 0, tiled=True, axis_index_groups=groups_of(size)
    )
    return moved.sum(0)


def collected(piece):
    size = lax.axis_size("row")
    core = lax.axis_index("row") % 2
    copies = jnp.broadcast_to(piece[None], (size // 2,) + piece.shape)
    own = lax.all_to_all(copies, "row", 0, 0, tiled=True, axis_index_groups=groups_of(size))
    other = swapped(own, "row", 1)
    return jnp.where(core == 0, jnp.stack([own, other]), jnp.stack([other, own]))


def pieces_of(gram):
    size = lax.axis_size("row")
    return gram.reshape(2, size // 2, -1, gram.shape[-1])


def body(leaves, level_one, level_two):
    rows = lax.axis_size("row")
    rank = leaves.shape[-1]
    node = lax.axis_index("node") % 2
    is_left = node == 0
    raw_two = level_two[0]
    sibling_two = swapped(raw_two, "node", 1)

    leaf_grams = jnp.einsum("nrc,nrd->ncd", leaves, leaves, precision=PRECISE)
    by_device = leaf_grams.reshape(2, 2, rows // 2, -1, rank).transpose(1, 2, 0, 3, 4)
    piece = scattered(by_device.reshape(2, rows // 2, -1, rank))
    full = collected(piece).reshape(2, rows // 2, 2, -1, rank).transpose(2, 0, 1, 3, 4)
    leaf_grams = full.reshape(2, rank, rank)
    leaf_scale = 1.0 / (leaves.shape[1] * rows)
    right_upper, right_inverse = factored(leaf_grams[1], leaf_scale)

    slab = level_one[0]
    depth = slab.shape[0]
    turned = jnp.einsum("jb,abk->ajk", right_upper, slab, precision=FAST)
    gathered = lax.all_to_all(turned, "row", split_axis=1, concat_axis=0, tiled=True)

    left_upper, left_inverse = factored(leaf_grams[0], leaf_scale)
    leaf_inverse = jnp.stack([left_inverse, right_inverse])
    leaf_bases = jnp.einsum("nrc,ndc->nrd", leaves, leaf_inverse, precision=FAST)

    moved_one = jnp.einsum("ia,ajk->ijk", left_upper, gathered, precision=FAST)
    flat_one = moved_one.reshape(-1, rank)
    one_gram = jnp.einsum("rc,rd->cd", flat_one, flat_one, precision=PRECISE)
    piece = scattered(pieces_of(one_gram))
    partner = swapped(piece, "node", 1)
    first = jnp.where(is_left, piece, partner)
    second = jnp.where(is_left, partner, piece)
    full = collected(jnp.stack([first, second])).transpose(2, 0, 1, 3, 4)
    one_grams = full.reshape(2, rank, rank)
    scale = 1.0 / (rank * rank)
    second_upper, second_inverse = factored(one_grams[1], scale)

    chosen = pick(second_upper.reshape(rows, 2, -1, rank).transpose(1, 0, 2, 3), node)
    chosen = chosen.reshape(-1, rank)
    pair = jnp.stack([raw_two, sibling_two], axis=1)
    pair = jnp.where(is_left, pair, pair[:, ::-1])
    pair = pair.reshape(-1, rank, rank)
    turned_two = jnp.einsum("jb,abk->ajk", chosen, pair, precision=FAST)
    gathered_two = lax.all_to_all(turned_two, "row", split_axis=1, concat_axis=0, tiled=True)

    first_upper, first_inverse = factored(one_grams[0], scale)
    one_inverse = jnp.where(is_left, first_inverse, second_inverse)
    level_one_bases = jnp.einsum("rc,dc->rd", flat_one, one_inverse, precision=FAST)
    level_one_bases = level_one_bases.reshape(moved_one.shape)[None]

    moved_two = jnp.einsum("ia,ajk->ijk", first_upper, gathered_two, precision=FAST)
    flat_two = moved_two.reshape(-1, rank)
    two_gram = jnp.einsum("rc,rd->cd", flat_two, flat_two, precision=PRECISE)
    by_parity = moved_two.reshape((rank // 2, 2) + moved_two.shape[1:])
    kept = jnp.where(is_left, by_parity[:, 0], by_parity[:, 1])
    sent = jnp.where(is_left, by_parity[:, 1], by_parity[:, 0])
    received = swapped(sent, "node", 1)
    piece = scattered(pieces_of(two_gram))
    piece = piece + swapped(piece, "node", 1)
    two_gram = collected(piece).reshape(rank, rank)
    two_upper, two_inverse = factored(two_gram, scale)
    whole_two = jnp.where(
        is_left,
        jnp.concatenate([kept, received], axis=1),
        jnp.concatenate([received, kept], axis=1),
    )
    level_two_bases = jnp.einsum("ijk,lk->ijl", whole_two, two_inverse, precision=FAST)[None]
    return (leaf_bases, level_one_bases, level_two_bases, two_upper[None])


def solution(mesh):
    placed = (P("node", "row", None), P("node", "row", None, None), P("node", "row", None, None))
    return jax.shard_map(
        body,
        mesh=mesh,
        in_specs=placed,
        out_specs=(
            P("node", "row", None),
            P("node", None, "row", None),
            P("node", None, "row", None),
            P("node", None, None),
        ),
        check_vma=False,
    )
```

```python
import functools
import jax
import jax.numpy as jnp
from jax import lax
from jax.experimental import pallas as pl
from jax.experimental.pallas import tpu as pltpu
from jax.sharding import PartitionSpec as P

FAST = lax.Precision.HIGH
SUB = 8
LANE = 128
DEPTH = 2
WHOLE = pl.BlockSpec(memory_space=pltpu.VMEM)
SCALARS = pl.BlockSpec(memory_space=pltpu.SMEM)
LIMIT = pltpu.CompilerParams(vmem_limit_bytes=48 * 2**20)


def floats(*shape):
    return jax.ShapeDtypeStruct(shape, jnp.float32)


def swapped(value, axis, mask):
    pairs = [(source, source ^ mask) for source in range(lax.axis_size(axis))]
    return lax.ppermute(value, axis, pairs)


def split(value):
    high = value.astype(jnp.bfloat16)
    return high, (value - high.astype(jnp.float32)).astype(jnp.bfloat16)


def product(left, right, dims):
    def dot(one, other):
        return lax.dot_general(one, other, (dims, ((), ())), preferred_element_type=jnp.float32)

    return dot(left[0], right[0]) + (dot(left[0], right[1]) + dot(left[1], right[0]))


def gram_terms(value):
    high, low = split(value)
    both = jnp.concatenate([high, low], axis=1)
    return lax.dot_general(
        high, both, (((0,), (0,)), ((), ())), preferred_element_type=jnp.float32
    )


def gram_of(terms):
    n = terms.shape[0]
    return terms[:, :n] + (terms[:, n:] + terms[:, n:].T)


def halves(gram_ref, core, kept_ref, sent_ref, put):
    half = gram_ref.shape[0] // 2
    kept = gram_ref[pl.ds(pl.multiple_of(core * half, half), half), :]
    sent = gram_ref[pl.ds(pl.multiple_of((1 - core) * half, half), half), :]
    put(kept_ref, kept)
    put(sent_ref, sent)


def leaf_kernel(place_ref, leaves_ref, kept_ref, sent_ref, gram_ref):
    count, rows, n = leaves_ref.shape
    step = min(rows, 256)
    for leaf in range(count):
        terms = jnp.zeros((n, 2 * n), jnp.float32)
        for start in range(0, rows, step):
            terms = terms + gram_terms(leaves_ref[leaf, start : start + step, :])
        gram_ref[...] = gram_of(terms)

        def put(ref, value):
            ref[:, leaf] = value.reshape(ref.shape[0], ref.shape[2], ref.shape[3])

        halves(gram_ref, place_ref[0], kept_ref, sent_ref, put)


def leaf_partials(place, leaves, chips):
    count, _, n = leaves.shape
    half = floats(chips, count, n // (2 * chips), n)
    return pl.pallas_call(
        leaf_kernel,
        in_specs=[SCALARS, WHOLE],
        out_specs=(WHOLE, WHOLE),
        out_shape=(half, half),
        scratch_shapes=[pltpu.VMEM((n, n), jnp.float32)],
        compiler_params=LIMIT,
        name="leaf_partials",
    )(place, leaves)


def factor_kernel(scale, place_ref, own_ref, other_ref, u_ref, v_ref, w_ref):
    n = u_ref.shape[0]
    chips, _, piece, _ = own_ref.shape
    core = place_ref[0]
    which = place_ref[1]
    for ref, half in ((own_ref, core), (other_ref, 1 - core)):
        for chip in range(chips):
            row = pl.multiple_of(half * (n // 2), n // 2) + chip * piece
            w_ref[pl.ds(row, piece), :n] = ref[chip, which] * scale
    ri = lax.broadcasted_iota(jnp.int32, (n, n), 0)
    ci = lax.broadcasted_iota(jnp.int32, (n, n), 1)
    w_ref[:, n:] = jnp.where(ri == ci, 1.0, 0.0)
    full=(SUB,LANE)
    sub=lax.broadcasted_iota(jnp.int32,full,0)
    lane=lax.broadcasted_iota(jnp.int32,full,1)
    zero=jnp.zeros(full,jnp.float32)
    def span(k): return (k//LANE)*LANE, n+((k+SUB+LANE-1)//LANE)*LANE
    def lanebc(x,o): return jnp.broadcast_to(x[:,o:o+1],full)
    def subbc(x,i): return jnp.broadcast_to(x[i:i+1,:],full)
    def load(k):
        lo,hi=span(k)
        P={t: w_ref[k:k+SUB,t*LANE:(t+1)*LANE] for t in range(lo//LANE,hi//LANE)}
        diag={}
        for j in range(SUB):
            c=lanebc(P[lo//LANE],k-lo+j)
            for i in range(j+1): diag[i,j]=subbc(c,i)
        return P,diag
    def loadp(k):
        lo,hi=span(k)
        return {t: w_ref[k:k+SUB,t*LANE:(t+1)*LANE] for t in range(lo//LANE,hi//LANE)}
    def diagof(P,k):
        diag={}
        for j in range(SUB):
            c=lanebc(P[k//LANE],k%LANE+j)
            for i in range(j+1): diag[i,j]=subbc(c,i)
        return diag
    def split3(x):
        h=x.astype(jnp.bfloat16); x=x-h.astype(jnp.float32)
        m=x.astype(jnp.bfloat16); x=x-m.astype(jnp.float32)
        return h,m,x.astype(jnp.bfloat16)
    coming={k: loadp(k) for k in range(0,min(DEPTH*SUB,n),SUB)}
    diag=diagof(coming[0],0)
    for k in range(0,n,SUB):
        lo,hi=span(k)
        tiles=range(lo//LANE,hi//LANE)
        nxt=k+SUB
        P=coming.pop(k)
        if nxt<n: ndiag=diagof(coming[nxt],nxt) if DEPTH>1 else None
        roots=zero
        for i in range(SUB):
            r=lax.rsqrt(diag[i,i])
            roots=jnp.where(sub==i,r,roots)
            if i<SUB-1:
                col=zero
                for j in range(i+1,SUB): col=jnp.where(sub==j,diag[i,j],col)
                col=col*(r*r)
                s={j: diag[i,j]*r for j in range(i+1,SUB)}
                for j in range(i+1,SUB):
                    for l in range(j,SUB): diag[j,l]=diag[j,l]-s[j]*s[l]
                for t in tiles: P[t]=P[t]-col*subbc(P[t],i)
        t0=lo//LANE
        done={t: P[t]*roots for t in tiles}
        done[t0]=jnp.where(lane>=(k-lo)+sub,done[t0],0.0)
        far=k+DEPTH*SUB
        if far<n: coming[far]=loadp(far)
        if nxt<n:
            tn,on=nxt//LANE,nxt%LANE
            E=[lanebc(done[tn],on+j) for j in range(SUB)]
            for i in range(SUB):
                for j in range(i,SUB):
                    ndiag[i,j]=ndiag[i,j]-jnp.broadcast_to(jnp.sum(E[i]*E[j],axis=0,keepdims=True),full)
            for kk in range(SUB):
                row={t: subbc(done[t],kk) for t in done}
                for q in coming:
                    tq,oq=q//LANE,q%LANE
                    c=jnp.sum(jnp.where(lane==oq+sub,row[tq],0.0),axis=1,keepdims=True)
                    c=jnp.broadcast_to(c,full)
                    for t in row:
                        if t in coming[q]: coming[q][t]=coming[q][t]-c*row[t]
        U=jnp.concatenate([done[t] for t in tiles],axis=1)
        if lo: u_ref[k:k+SUB,:lo]=jnp.zeros((SUB,lo),jnp.float32)
        u_ref[k:k+SUB,lo:]=U[:,:n-lo]
        v_ref[k:k+SUB,:hi-n]=U[:,n-lo:]
        if hi<2*n: v_ref[k:k+SUB,hi-n:]=jnp.zeros((SUB,2*n-hi),jnp.float32)
        below=far+SUB
        if below<n:
            lane1=(below//LANE)*LANE
            h,m,l=split3(U[:,lane1-lo:])
            lhs=jnp.concatenate([x[:,:n-lane1].astype(jnp.float32) for x in (h,h,m,h,l,m)],axis=0).astype(jnp.bfloat16)
            rhs=jnp.concatenate([x.astype(jnp.float32) for x in (h,m,h,l,h,m)],axis=0).astype(jnp.bfloat16)
            M=lax.dot_general(lhs,rhs,(((0,),(0,)),((),())),preferred_element_type=jnp.float32)
            w_ref[below:, lane1:hi]=w_ref[below:, lane1:hi]-M[below-lane1:,:]
        if nxt<n: diag=ndiag


def factored(place, own, other, scale):
    n = own.shape[-1]
    return pl.pallas_call(
        functools.partial(factor_kernel, scale),
        in_specs=[SCALARS, WHOLE, WHOLE],
        out_specs=(WHOLE, WHOLE),
        out_shape=(floats(n, n), floats(n, n)),
        scratch_shapes=[pltpu.VMEM((n, 2 * n), jnp.float32)],
        compiler_params=LIMIT,
        name="factor",
    )(place, own, other)


def turn_kernel(factor_ref, *refs):
    factor = split(factor_ref[...])
    out_ref = refs[-1]
    for which, slab_ref in enumerate(refs[:-1]):
        for a in range(slab_ref.shape[0]):
            turned = product(factor, split(slab_ref[a]), ((1,), (0,)))
            out_ref[:, which, a] = turned.reshape(
                out_ref.shape[0], out_ref.shape[3], out_ref.shape[4]
            )


def turned_by(factor, slabs, dests):
    depth, n, _ = slabs[0].shape
    cols = factor.shape[0] // dests
    if cols % SUB:
        stacked = jnp.stack(slabs)
        moved = jnp.einsum("djb,sabk->dsajk", factor.reshape(dests, cols, n), stacked, precision=FAST)
        return moved
    step = max(1, 4 // len(slabs))
    step = step if depth % step == 0 else 1
    return pl.pallas_call(
        turn_kernel,
        grid=(depth // step,),
        in_specs=[pl.BlockSpec(factor.shape, lambda g: (0, 0))]
        + [pl.BlockSpec((step, n, n), lambda g: (g, 0, 0))] * len(slabs),
        out_specs=pl.BlockSpec((dests, len(slabs), step, cols, n), lambda g: (0, 0, g, 0, 0)),
        out_shape=floats(dests, len(slabs), depth, cols, n),
        compiler_params=LIMIT,
        name="turn",
    )(factor, *slabs)


def move_kernel(place_ref, factor_ref, x_ref, y_ref, *refs):
    moved_refs, (kept_ref, sent_ref, terms_ref, gram_ref) = refs[:-4], refs[-4:]
    step = pl.program_id(0)

    @pl.when(step == 0)
    def _():
        terms_ref[...] = jnp.zeros_like(terms_ref)

    factor = split(factor_ref[...])
    depth, cols, lanes = x_ref.shape
    flat = [ref.reshape(depth * cols, lanes) for ref in (x_ref, y_ref)]
    terms = terms_ref[...]
    for s in range(cols):
        parts = [ref[pl.ds(s, depth, stride=cols), :] for ref in flat]
        moved = product(factor, split(jnp.concatenate(parts, axis=1)), ((1,), (0,)))
        rows = depth // len(moved_refs)
        for which, ref in enumerate(moved_refs):
            ref[s] = moved[which * rows : (which + 1) * rows]
        terms = terms + gram_terms(moved)
    terms_ref[...] = terms

    @pl.when(step == pl.num_programs(0) - 1)
    def _():
        gram_ref[...] = gram_of(terms)

        def put(ref, value):
            ref[...] = value.reshape(ref.shape)

        halves(gram_ref, place_ref[0], kept_ref, sent_ref, put)


def moved_by(place, factor, gathered, chips, outputs):
    depth, cols, n = gathered.shape
    half = floats(chips, 1, n // (2 * chips), n)
    if cols % SUB:
        moved = jnp.einsum("ia,ajk->jik", factor, gathered, precision=FAST)
        flat = moved.reshape(-1, n)
        gram = jnp.einsum("rc,rd->cd", flat, flat, precision=lax.Precision.HIGHEST)
        both = gram.reshape((2,) + half.shape)
        core = place[0]
        return (
            *jnp.split(moved, outputs, axis=1),
            lax.dynamic_index_in_dim(both, core, 0, keepdims=False),
            lax.dynamic_index_in_dim(both, 1 - core, 0, keepdims=False),
        )
    rows = depth // outputs
    return pl.pallas_call(
        move_kernel,
        grid=(cols // SUB,),
        in_specs=[
            SCALARS,
            pl.BlockSpec(factor.shape, lambda g: (0, 0)),
            pl.BlockSpec((depth, SUB, n // 2), lambda g: (0, g, 0)),
            pl.BlockSpec((depth, SUB, n // 2), lambda g: (0, g, 1)),
        ],
        out_specs=[pl.BlockSpec((SUB, rows, n), lambda g: (g, 0, 0))] * outputs
        + [pl.BlockSpec(half.shape, lambda g: (0, 0, 0, 0))] * 2,
        out_shape=[floats(cols, rows, n)] * outputs + [half, half],
        scratch_shapes=[pltpu.VMEM((n, 2 * n), jnp.float32), pltpu.VMEM((n, n), jnp.float32)],
        compiler_params=LIMIT,
        name="move",
    )(place, factor, gathered, gathered)


def base_kernel(inverse_ref, moved_ref, out_ref):
    inverse = split(inverse_ref[...])
    cols, rows, _ = moved_ref.shape
    flat = out_ref.reshape(rows * cols, out_ref.shape[2])
    for s in range(cols):
        flat[pl.ds(s, rows, stride=cols), :] = product(split(moved_ref[s]), inverse, ((1,), (1,)))


def bases_of(inverse, moved):
    cols, rows, n = moved.shape
    if cols % SUB:
        return jnp.einsum("jik,lk->ijl", moved, inverse, precision=FAST)
    return pl.pallas_call(
        base_kernel,
        grid=(cols // SUB, 2),
        in_specs=[
            pl.BlockSpec((n // 2, n), lambda g, h: (h, 0)),
            pl.BlockSpec((SUB, rows, n), lambda g, h: (g, 0, 0)),
        ],
        out_specs=pl.BlockSpec((rows, SUB, n // 2), lambda g, h: (0, g, h)),
        out_shape=floats(rows, cols, n),
        compiler_params=LIMIT,
        name="bases",
    )(inverse, moved)


def groups_of(size):
    return [list(range(0, size, 2)), list(range(1, size, 2))]


def scattered(kept, sent):
    both = kept + swapped(sent, "row", 1)
    groups = groups_of(lax.axis_size("row"))
    return lax.all_to_all(both, "row", 0, 0, tiled=True, axis_index_groups=groups).sum(0)


def collected(piece):
    size = lax.axis_size("row")
    copies = jnp.broadcast_to(piece[None], (size // 2,) + piece.shape)
    own = lax.all_to_all(copies, "row", 0, 0, tiled=True, axis_index_groups=groups_of(size))
    return own, swapped(own, "row", 1)


def body(leaves, level_one, level_two):
    rows = lax.axis_size("row")
    chips = rows // 2
    rank = leaves.shape[-1]
    node = lax.axis_index("node") % 2
    is_left = node == 0
    core = lax.axis_index("row") % 2

    def place(which):
        return jnp.stack([core, jnp.int32(which)]).astype(jnp.int32)

    own_two = level_two[0]
    sibling_two = swapped(own_two, "node", 1)

    leaf_piece = scattered(*leaf_partials(place(0), leaves, chips))
    leaf_grams = collected(leaf_piece)
    leaf_scale = 1.0 / (leaves.shape[1] * rows)
    right_upper, right_inverse = factored(place(1), *leaf_grams, leaf_scale)
    turned = turned_by(right_upper, [level_one[0]], rows)
    gathered = lax.all_to_all(turned, "row", 0, 0, tiled=True)

    left_upper, left_inverse = factored(place(0), *leaf_grams, leaf_scale)
    leaf_inverse = jnp.stack([left_inverse, right_inverse])
    leaf_bases = jnp.einsum("nrc,ndc->nrd", leaves, leaf_inverse, precision=FAST)
    gathered, leaf_bases = lax.optimization_barrier((gathered, leaf_bases))

    cols = gathered.shape[3]
    moved_one, kept, sent = moved_by(
        place(0), left_upper, gathered.reshape(rank, cols, rank), chips, 1
    )
    one_piece = scattered(kept, sent)
    one_pieces = jnp.concatenate([one_piece, swapped(one_piece, "node", 1)])
    one_grams = collected(one_pieces)
    scale = 1.0 / (rank * rank)
    right_upper, right_inverse = factored(place(1 - node), *one_grams, scale)

    chosen = right_upper.reshape(rows, 2, -1, rank).transpose(1, 0, 2, 3)
    chosen = lax.dynamic_index_in_dim(chosen, node, 0, keepdims=False).reshape(-1, rank)
    turned = turned_by(chosen, [own_two, sibling_two], rows)
    gathered = lax.all_to_all(turned, "row", 0, 0, tiled=True)

    left_upper, left_inverse = factored(place(node), *one_grams, scale)
    one_inverse = jnp.where(is_left, left_inverse, right_inverse)
    level_one_bases = bases_of(one_inverse, moved_one)[None]
    depth = own_two.shape[0]
    sorted_left = left_upper.reshape(rank // 2, 2, rows, depth, 2).transpose(1, 0, 2, 4, 3)
    sorted_left = jnp.where(is_left, sorted_left, sorted_left[::-1, :, :, ::-1])
    sorted_left = sorted_left.reshape(rank, rank)
    gathered, level_one_bases, sorted_left = lax.optimization_barrier(
        (gathered, level_one_bases, sorted_left)
    )

    cols = gathered.shape[3]
    mine, theirs, kept, sent = moved_by(
        place(0), sorted_left, gathered.reshape(rank, cols, rank), chips, 2
    )
    two_piece = scattered(kept, sent)
    two_partner = swapped(two_piece, "node", 1)
    theirs, two_partner = lax.optimization_barrier((theirs, two_partner))
    received = swapped(theirs, "node", 1)
    two_gram = collected(two_piece + two_partner)
    two_upper, two_inverse = factored(place(0), *two_gram, scale)
    whole_two = jnp.where(
        is_left, jnp.concatenate([mine, received]), jnp.concatenate([received, mine])
    )
    level_two_bases = bases_of(two_inverse, whole_two)[None]
    return (leaf_bases, level_one_bases, level_two_bases, two_upper[None])


def solution(mesh):
    placed = (P("node", "row", None), P("node", "row", None, None), P("node", "row", None, None))
    return jax.shard_map(
        body,
        mesh=mesh,
        in_specs=placed,
        out_specs=(
            P("node", "row", None),
            P("node", None, "row", None),
            P("node", None, "row", None),
            P("node", None, None),
        ),
        check_vma=False,
    )
```

```python
import functools
import jax
import jax.numpy as jnp
from jax import lax
from jax.experimental import pallas as pl
from jax.experimental.pallas import tpu as pltpu
from jax.sharding import PartitionSpec as P

FAST = lax.Precision.HIGH
SUB = 8
LANE = 128
DEPTH = 2
WHOLE = pl.BlockSpec(memory_space=pltpu.VMEM)
SCALARS = pl.BlockSpec(memory_space=pltpu.SMEM)
LIMIT = pltpu.CompilerParams(vmem_limit_bytes=48 * 2**20)


def floats(*shape):
    return jax.ShapeDtypeStruct(shape, jnp.float32)


def swapped(value, axis, mask):
    pairs = [(source, source ^ mask) for source in range(lax.axis_size(axis))]
    return lax.ppermute(value, axis, pairs)


def split(value):
    high = value.astype(jnp.bfloat16)
    return high, (value - high.astype(jnp.float32)).astype(jnp.bfloat16)


def product(left, right, dims):
    def dot(one, other):
        return lax.dot_general(one, other, (dims, ((), ())), preferred_element_type=jnp.float32)

    return dot(left[0], right[0]) + (dot(left[0], right[1]) + dot(left[1], right[0]))


def gram_terms(value):
    high, low = split(value)
    both = jnp.concatenate([high, low], axis=1)
    return lax.dot_general(
        high, both, (((0,), (0,)), ((), ())), preferred_element_type=jnp.float32
    )


def gram_of(terms):
    n = terms.shape[0]
    return terms[:, :n] + (terms[:, n:] + terms[:, n:].T)


def packed(gram, core):
    half, quarter = gram.shape[0] // 2, gram.shape[0] // 4
    if core == 0:
        square, row, corner = gram[:quarter, :half], gram[:quarter, half:], gram[-quarter:, -quarter:]
    else:
        square, row = gram[half : half + quarter, half:], gram[quarter:half, half:]
        corner = gram[quarter:half, quarter:half]
    corner = jnp.concatenate([corner[: quarter // 2], corner[quarter // 2 :]], axis=1)
    return jnp.concatenate([square, row, corner], axis=0)


def packed_shape(n):
    return floats(n // 4 * 2 + n // 8, n // 2)


def put_parts(gram, core, kept_ref, sent_ref):
    first, second = packed(gram, 0), packed(gram, 1)
    kept_ref[...] = jnp.where(core == 0, first, second)
    sent_ref[...] = jnp.where(core == 0, second, first)


def leaf_kernel(place_ref, leaf_ref, kept_ref, sent_ref):
    _, rows, n = leaf_ref.shape
    step = min(rows, 256)
    terms = jnp.zeros((n, 2 * n), jnp.float32)
    for start in range(0, rows, step):
        terms = terms + gram_terms(leaf_ref[0, start : start + step, :])
    put_parts(gram_of(terms), place_ref[0], kept_ref, sent_ref)


def leaf_partial(place, leaves, leaf):
    _, rows, n = leaves.shape
    part = packed_shape(n)
    return pl.pallas_call(
        leaf_kernel,
        grid=(1,),
        in_specs=[SCALARS, pl.BlockSpec((1, rows, n), lambda g: (leaf, 0, 0))],
        out_specs=(pl.BlockSpec(part.shape, lambda g: (0, 0)),) * 2,
        out_shape=(part, part),
        compiler_params=LIMIT,
        name="leaf_partial",
    )(place, leaves)


def leaf_base_kernel(leaf_ref, first_ref, second_ref, out_ref):
    for leaf, ref in enumerate((first_ref, second_ref)):
        inverse = split(ref[...])
        out_ref[leaf] = product(split(leaf_ref[leaf]), inverse, ((1,), (1,)))


def leaf_bases_of(leaves, first, second):
    count, rows, n = leaves.shape
    step = min(rows, 256)
    return pl.pallas_call(
        leaf_base_kernel,
        grid=(rows // step,),
        in_specs=[pl.BlockSpec((count, step, n), lambda g: (0, g, 0))]
        + [pl.BlockSpec((n, n), lambda g: (0, 0))] * 2,
        out_specs=pl.BlockSpec((count, step, n), lambda g: (0, g, 0)),
        out_shape=floats(count, rows, n),
        compiler_params=LIMIT,
        name="leaf_bases",
    )(leaves, first, second)


def factor_kernel(scale, place_ref, own_ref, other_ref, u_ref, v_ref, w_ref):
    n = u_ref.shape[0]
    half, quarter = n // 2, n // 4
    own, other = own_ref[...] * scale, other_ref[...] * scale
    mine = place_ref[0] == 0
    w_ref[:, :n] = jnp.zeros((n, n), jnp.float32)
    for core, part in ((0, jnp.where(mine, own, other)), (1, jnp.where(mine, other, own))):
        square, row, corner = part[:quarter], part[quarter:half], part[half:]
        corner = jnp.concatenate([corner[:, :quarter], corner[:, quarter:]], axis=0)
        start = core * half
        w_ref[start : start + quarter, start : start + half] = square
        w_ref[core * quarter : (core + 1) * quarter, half:n] = row
        start = n - quarter if core == 0 else quarter
        w_ref[start : start + quarter, start : start + quarter] = corner
    ri = lax.broadcasted_iota(jnp.int32, (n, n), 0)
    ci = lax.broadcasted_iota(jnp.int32, (n, n), 1)
    w_ref[:, n:] = jnp.where(ri == ci, 1.0, 0.0)
    full=(SUB,LANE)
    sub=lax.broadcasted_iota(jnp.int32,full,0)
    lane=lax.broadcasted_iota(jnp.int32,full,1)
    zero=jnp.zeros(full,jnp.float32)
    def span(k): return (k//LANE)*LANE, n+((k+SUB+LANE-1)//LANE)*LANE
    def lanebc(x,o): return jnp.broadcast_to(x[:,o:o+1],full)
    def subbc(x,i): return jnp.broadcast_to(x[i:i+1,:],full)
    def load(k):
        lo,hi=span(k)
        P={t: w_ref[k:k+SUB,t*LANE:(t+1)*LANE] for t in range(lo//LANE,hi//LANE)}
        diag={}
        for j in range(SUB):
            c=lanebc(P[lo//LANE],k-lo+j)
            for i in range(j+1): diag[i,j]=subbc(c,i)
        return P,diag
    def loadp(k):
        lo,hi=span(k)
        return {t: w_ref[k:k+SUB,t*LANE:(t+1)*LANE] for t in range(lo//LANE,hi//LANE)}
    def diagof(P,k):
        diag={}
        for j in range(SUB):
            c=lanebc(P[k//LANE],k%LANE+j)
            for i in range(j+1): diag[i,j]=subbc(c,i)
        return diag
    def split3(x):
        h=x.astype(jnp.bfloat16); x=x-h.astype(jnp.float32)
        m=x.astype(jnp.bfloat16); x=x-m.astype(jnp.float32)
        return h,m,x.astype(jnp.bfloat16)
    coming={k: loadp(k) for k in range(0,min(DEPTH*SUB,n),SUB)}
    diag=diagof(coming[0],0)
    for k in range(0,n,SUB):
        lo,hi=span(k)
        tiles=range(lo//LANE,hi//LANE)
        nxt=k+SUB
        P=coming.pop(k)
        if nxt<n: ndiag=diagof(coming[nxt],nxt) if DEPTH>1 else None
        roots=zero
        for i in range(SUB):
            r=lax.rsqrt(diag[i,i])
            roots=jnp.where(sub==i,r,roots)
            if i<SUB-1:
                col=zero
                for j in range(i+1,SUB): col=jnp.where(sub==j,diag[i,j],col)
                col=col*(r*r)
                s={j: diag[i,j]*r for j in range(i+1,SUB)}
                for j in range(i+1,SUB):
                    for l in range(j,SUB): diag[j,l]=diag[j,l]-s[j]*s[l]
                for t in tiles: P[t]=P[t]-col*subbc(P[t],i)
        t0=lo//LANE
        done={t: P[t]*roots for t in tiles}
        done[t0]=jnp.where(lane>=(k-lo)+sub,done[t0],0.0)
        far=k+DEPTH*SUB
        if far<n: coming[far]=loadp(far)
        if nxt<n:
            tn,on=nxt//LANE,nxt%LANE
            E=[lanebc(done[tn],on+j) for j in range(SUB)]
            for i in range(SUB):
                for j in range(i,SUB):
                    ndiag[i,j]=ndiag[i,j]-jnp.broadcast_to(jnp.sum(E[i]*E[j],axis=0,keepdims=True),full)
            for kk in range(SUB):
                row={t: subbc(done[t],kk) for t in done}
                for q in coming:
                    tq,oq=q//LANE,q%LANE
                    c=jnp.sum(jnp.where(lane==oq+sub,row[tq],0.0),axis=1,keepdims=True)
                    c=jnp.broadcast_to(c,full)
                    for t in row:
                        if t in coming[q]: coming[q][t]=coming[q][t]-c*row[t]
        U=jnp.concatenate([done[t] for t in tiles],axis=1)
        if lo: u_ref[k:k+SUB,:lo]=jnp.zeros((SUB,lo),jnp.float32)
        u_ref[k:k+SUB,lo:]=U[:,:n-lo]
        v_ref[k:k+SUB,:hi-n]=U[:,n-lo:]
        if hi<2*n: v_ref[k:k+SUB,hi-n:]=jnp.zeros((SUB,2*n-hi),jnp.float32)
        below=far+SUB
        if below<n:
            lane1=(below//LANE)*LANE
            h,m,l=split3(U[:,lane1-lo:])
            lhs=jnp.concatenate([x[:,:n-lane1].astype(jnp.float32) for x in (h,h,m,h,l,m)],axis=0).astype(jnp.bfloat16)
            rhs=jnp.concatenate([x.astype(jnp.float32) for x in (h,m,h,l,h,m)],axis=0).astype(jnp.bfloat16)
            M=lax.dot_general(lhs,rhs,(((0,),(0,)),((),())),preferred_element_type=jnp.float32)
            w_ref[below:, lane1:hi]=w_ref[below:, lane1:hi]-M[below-lane1:,:]
        if nxt<n: diag=ndiag


def factored(place, own, other, scale):
    n = own.shape[-1] * 2
    return pl.pallas_call(
        functools.partial(factor_kernel, scale),
        in_specs=[SCALARS, WHOLE, WHOLE],
        out_specs=(WHOLE, WHOLE),
        out_shape=(floats(n, n), floats(n, n)),
        scratch_shapes=[pltpu.VMEM((n, 2 * n), jnp.float32)],
        compiler_params=LIMIT,
        name="factor",
    )(place, own, other)


def turn_kernel(factor_ref, *refs):
    factor = split(factor_ref[...])
    out_ref = refs[-1]
    for which, slab_ref in enumerate(refs[:-1]):
        for a in range(slab_ref.shape[0]):
            turned = product(factor, split(slab_ref[a]), ((1,), (0,)))
            out_ref[:, which, a] = turned.reshape(
                out_ref.shape[0], out_ref.shape[3], out_ref.shape[4]
            )


def turned_by(factor, slabs, dests):
    depth, n, _ = slabs[0].shape
    cols = factor.shape[0] // dests
    if cols % SUB:
        stacked = jnp.stack(slabs)
        moved = jnp.einsum("djb,sabk->dsajk", factor.reshape(dests, cols, n), stacked, precision=FAST)
        return moved
    step = max(1, 4 // len(slabs))
    step = step if depth % step == 0 else 1
    return pl.pallas_call(
        turn_kernel,
        grid=(depth // step,),
        in_specs=[pl.BlockSpec(factor.shape, lambda g: (0, 0))]
        + [pl.BlockSpec((step, n, n), lambda g: (g, 0, 0))] * len(slabs),
        out_specs=pl.BlockSpec((dests, len(slabs), step, cols, n), lambda g: (0, 0, g, 0, 0)),
        out_shape=pltpu.HBM((dests, len(slabs), depth, cols, n), jnp.float32),
        compiler_params=LIMIT,
        name="turn",
    )(factor, *slabs)


def move_kernel(place_ref, factor_ref, x_ref, y_ref, *refs):
    moved_refs, (kept_ref, sent_ref, terms_ref) = refs[:-3], refs[-3:]
    step = pl.program_id(0)

    @pl.when(step == 0)
    def _():
        terms_ref[...] = jnp.zeros_like(terms_ref)

    factor = split(factor_ref[...])
    depth, cols, lanes = x_ref.shape
    flat = [ref.reshape(depth * cols, lanes) for ref in (x_ref, y_ref)]
    terms = terms_ref[...]
    for s in range(cols):
        parts = [ref[pl.ds(s, depth, stride=cols), :] for ref in flat]
        moved = product(factor, split(jnp.concatenate(parts, axis=1)), ((1,), (0,)))
        rows = depth // len(moved_refs)
        for which, ref in enumerate(moved_refs):
            ref[s] = moved[which * rows : (which + 1) * rows]
        terms = terms + gram_terms(moved)
    terms_ref[...] = terms

    @pl.when(step == pl.num_programs(0) - 1)
    def _():
        put_parts(gram_of(terms), place_ref[0], kept_ref, sent_ref)


def moved_by(place, factor, gathered, outputs):
    depth, cols, n = gathered.shape
    part = packed_shape(n)
    if cols % SUB:
        moved = jnp.einsum("ia,ajk->jik", factor, gathered, precision=FAST)
        flat = moved.reshape(-1, n)
        gram = jnp.einsum("rc,rd->cd", flat, flat, precision=lax.Precision.HIGHEST)
        parts = packed(gram, 0), packed(gram, 1)
        first = place[0] == 0
        kept, sent = jnp.where(first, *parts), jnp.where(first, *parts[::-1])
        return (*jnp.split(moved, outputs, axis=1), kept, sent)
    rows = depth // outputs
    return pl.pallas_call(
        move_kernel,
        grid=(cols // SUB,),
        in_specs=[
            SCALARS,
            pl.BlockSpec(factor.shape, lambda g: (0, 0)),
            pl.BlockSpec((depth, SUB, n // 2), lambda g: (0, g, 0)),
            pl.BlockSpec((depth, SUB, n // 2), lambda g: (0, g, 1)),
        ],
        out_specs=[pl.BlockSpec((SUB, rows, n), lambda g: (g, 0, 0))] * outputs
        + [pl.BlockSpec(part.shape, lambda g: (0, 0))] * 2,
        out_shape=[pltpu.HBM((cols, rows, n), jnp.float32)] * outputs + [part, part],
        scratch_shapes=[pltpu.VMEM((n, 2 * n), jnp.float32)],
        compiler_params=LIMIT,
        name="move",
    )(place, factor, gathered, gathered)


def base_kernel(inverse_ref, moved_ref, out_ref):
    inverse = split(inverse_ref[...])
    cols, rows, _ = moved_ref.shape
    flat = out_ref.reshape(rows * cols, out_ref.shape[2])
    for s in range(cols):
        flat[pl.ds(s, rows, stride=cols), :] = product(split(moved_ref[s]), inverse, ((1,), (1,)))


def bases_of(inverse, moved):
    cols, rows, n = moved.shape
    if cols % SUB:
        return jnp.einsum("jik,lk->ijl", moved, inverse, precision=FAST)
    return pl.pallas_call(
        base_kernel,
        grid=(cols // SUB, 2),
        in_specs=[
            pl.BlockSpec((n // 2, n), lambda g, h: (h, 0)),
            pl.BlockSpec((SUB, rows, n), lambda g, h: (g, 0, 0)),
        ],
        out_specs=pl.BlockSpec((rows, SUB, n // 2), lambda g, h: (0, g, h)),
        out_shape=floats(rows, cols, n),
        compiler_params=LIMIT,
        name="bases",
    )(inverse, moved)


def summed(kept, sent):
    total = kept + swapped(sent, "row", 1)
    mask = 2
    while mask < lax.axis_size("row"):
        total = total + swapped(total, "row", mask)
        mask *= 2
    return total


def sorted_by(factor, rows_from, cols_from):
    n = factor.shape[0]
    ids = jnp.arange(n, dtype=jnp.int32)
    high = lax.Precision.HIGHEST
    chosen = (ids[:, None] == cols_from[None, :]).astype(jnp.float32)
    factor = jnp.dot(factor, chosen, precision=high)
    chosen = (rows_from[:, None] == ids[None, :]).astype(jnp.float32)
    return jnp.dot(chosen, factor, precision=high)


def body(leaves, level_one, level_two):
    rows = lax.axis_size("row")
    rank = leaves.shape[-1]
    node = lax.axis_index("node") % 2
    is_left = node == 0
    place = jnp.stack([lax.axis_index("row") % 2]).astype(jnp.int32)

    def factors_of(part, scale):
        return factored(place, part, swapped(part, "row", 1), scale)

    own_two = level_two[0]
    sibling_two = swapped(own_two, "node", 1)

    leaf_scale = 1.0 / (leaves.shape[1] * rows)
    right_part = summed(*leaf_partial(place, leaves, 1))
    left_part = summed(*leaf_partial(place, leaves, 0))
    right_upper, right_inverse = factors_of(right_part, leaf_scale)
    turned = turned_by(right_upper, [level_one[0]], rows)
    gathered = lax.all_to_all(turned, "row", 0, 0, tiled=True)

    left_upper, left_inverse = factors_of(left_part, leaf_scale)
    leaf_bases = leaf_bases_of(leaves, left_inverse, right_inverse)
    gathered, leaf_bases = lax.optimization_barrier((gathered, leaf_bases))

    cols = gathered.shape[3]
    moved_one, kept, sent = moved_by(place, left_upper, gathered.reshape(rank, cols, rank), 1)
    own_part = summed(kept, sent)
    sibling_part = swapped(own_part, "node", 1)
    scale = 1.0 / (rank * rank)
    right_upper, right_inverse = factors_of(jnp.where(is_left, sibling_part, own_part), scale)

    chosen = right_upper.reshape(rows, 2, -1, rank).transpose(1, 0, 2, 3)
    chosen = lax.dynamic_index_in_dim(chosen, node, 0, keepdims=False).reshape(-1, rank)
    turned = turned_by(chosen, [own_two, sibling_two], rows)
    gathered = lax.all_to_all(turned, "row", 0, 0, tiled=True)

    left_upper, left_inverse = factors_of(jnp.where(is_left, own_part, sibling_part), scale)
    one_inverse = jnp.where(is_left, left_inverse, right_inverse)
    level_one_bases = bases_of(one_inverse, moved_one)[None]
    ids = jnp.arange(rank, dtype=jnp.int32)
    depth = own_two.shape[0]
    rows_from = 2 * (ids % (rank // 2)) + (ids // (rank // 2) + node) % 2
    cols_from = ids // (2 * depth) * (2 * depth) + 2 * (ids % depth) + (ids // depth + node) % 2
    sorted_left = sorted_by(left_upper, rows_from, cols_from)
    gathered, level_one_bases, sorted_left = lax.optimization_barrier(
        (gathered, level_one_bases, sorted_left)
    )

    cols = gathered.shape[3]
    mine, theirs, kept, sent = moved_by(place, sorted_left, gathered.reshape(rank, cols, rank), 2)
    row_part = summed(kept, sent)
    node_part = swapped(row_part, "node", 1)
    theirs, node_part = lax.optimization_barrier((theirs, node_part))
    received = swapped(theirs, "node", 1)
    two_upper, two_inverse = factors_of(row_part + node_part, scale)
    whole_two = jnp.where(
        is_left, jnp.concatenate([mine, received]), jnp.concatenate([received, mine])
    )
    level_two_bases = bases_of(two_inverse, whole_two)[None]
    return (leaf_bases, level_one_bases, level_two_bases, two_upper[None])


def solution(mesh):
    placed = (P("node", "row", None), P("node", "row", None, None), P("node", "row", None, None))
    return jax.shard_map(
        body,
        mesh=mesh,
        in_specs=placed,
        out_specs=(
            P("node", "row", None),
            P("node", None, "row", None),
            P("node", None, "row", None),
            P("node", None, None),
        ),
        check_vma=False,
    )
```

```python
import functools
import jax
import jax.numpy as jnp
from jax import lax
from jax.experimental import pallas as pl
from jax.experimental.pallas import tpu as pltpu
from jax.sharding import PartitionSpec as P

FAST = lax.Precision.HIGH
SUB = 8
LANE = 128
DEPTH = 2
WHOLE = pl.BlockSpec(memory_space=pltpu.VMEM)
SCALARS = pl.BlockSpec(memory_space=pltpu.SMEM)
LIMIT = pltpu.CompilerParams(vmem_limit_bytes=48 * 2**20)


def in_hbm(value):
    return pltpu.with_memory_space_constraint(value, pltpu.HBM)


def floats(*shape):
    return jax.ShapeDtypeStruct(shape, jnp.float32)


def swapped(value, axis, mask):
    pairs = [(source, source ^ mask) for source in range(lax.axis_size(axis))]
    return lax.ppermute(value, axis, pairs)


def split(value):
    high = value.astype(jnp.bfloat16)
    return high, (value - high.astype(jnp.float32)).astype(jnp.bfloat16)


def product(left, right, dims):
    def dot(one, other):
        return lax.dot_general(one, other, (dims, ((), ())), preferred_element_type=jnp.float32)

    if dims[0] == (1,):
        rows = left[0].shape[0]
        both = dot(jnp.concatenate(left, axis=0), right[0])
        return both[:rows] + (dot(left[0], right[1]) + both[rows:])
    return dot(left[0], right[0]) + (dot(left[0], right[1]) + dot(left[1], right[0]))


def gram_terms(value):
    high, low = split(value)
    both = jnp.concatenate([high, low], axis=1)
    return lax.dot_general(
        high, both, (((0,), (0,)), ((), ())), preferred_element_type=jnp.float32
    )


def gram_of(terms):
    n = terms.shape[0]
    return terms[:, :n] + (terms[:, n:] + terms[:, n:].T)


def packed(gram, core):
    half, quarter = gram.shape[0] // 2, gram.shape[0] // 4
    if core == 0:
        square, row, corner = gram[:quarter, :half], gram[:quarter, half:], gram[-quarter:, -quarter:]
    else:
        square, row = gram[half : half + quarter, half:], gram[quarter:half, half:]
        corner = gram[quarter:half, quarter:half]
    corner = jnp.concatenate([corner[: quarter // 2], corner[quarter // 2 :]], axis=1)
    return jnp.concatenate([square, row, corner], axis=0)


def packed_shape(n):
    return floats(n // 4 * 2 + n // 8, n // 2)


def put_parts(gram, core, kept_ref, sent_ref):
    first, second = packed(gram, 0), packed(gram, 1)
    kept_ref[...] = jnp.where(core == 0, first, second)
    sent_ref[...] = jnp.where(core == 0, second, first)


def leaf_kernel(place_ref, leaf_ref, kept_ref, sent_ref):
    _, rows, n = leaf_ref.shape
    step = min(rows, 256)
    terms = jnp.zeros((n, 2 * n), jnp.float32)
    for start in range(0, rows, step):
        terms = terms + gram_terms(leaf_ref[0, start : start + step, :])
    put_parts(gram_of(terms), place_ref[0], kept_ref, sent_ref)


def leaf_partial(place, leaves, leaf):
    _, rows, n = leaves.shape
    part = packed_shape(n)
    return pl.pallas_call(
        leaf_kernel,
        grid=(1,),
        in_specs=[SCALARS, pl.BlockSpec((1, rows, n), lambda g: (leaf, 0, 0))],
        out_specs=(pl.BlockSpec(part.shape, lambda g: (0, 0)),) * 2,
        out_shape=(part, part),
        compiler_params=LIMIT,
        name="leaf_partial",
    )(place, in_hbm(leaves))


def leaf_base_kernel(leaf_ref, first_ref, second_ref, out_ref):
    for leaf, ref in enumerate((first_ref, second_ref)):
        inverse = split(ref[...])
        out_ref[leaf] = product(split(leaf_ref[leaf]), inverse, ((1,), (1,)))


def leaf_bases_of(leaves, first, second):
    count, rows, n = leaves.shape
    step = min(rows, 256)
    return pl.pallas_call(
        leaf_base_kernel,
        grid=(rows // step,),
        in_specs=[pl.BlockSpec((count, step, n), lambda g: (0, g, 0))]
        + [pl.BlockSpec((n, n), lambda g: (0, 0))] * 2,
        out_specs=pl.BlockSpec((count, step, n), lambda g: (0, g, 0)),
        out_shape=floats(count, rows, n),
        compiler_params=LIMIT,
        name="leaf_bases",
    )(in_hbm(leaves), first, second)


def factor_kernel(scale, place_ref, own_ref, other_ref, u_ref, v_ref, w_ref):
    n = u_ref.shape[0]
    half, quarter = n // 2, n // 4
    own, other = own_ref[...] * scale, other_ref[...] * scale
    mine = place_ref[0] == 0
    w_ref[:, :n] = jnp.zeros((n, n), jnp.float32)
    for core, part in ((0, jnp.where(mine, own, other)), (1, jnp.where(mine, other, own))):
        square, row, corner = part[:quarter], part[quarter:half], part[half:]
        corner = jnp.concatenate([corner[:, :quarter], corner[:, quarter:]], axis=0)
        start = core * half
        w_ref[start : start + quarter, start : start + half] = square
        w_ref[core * quarter : (core + 1) * quarter, half:n] = row
        start = n - quarter if core == 0 else quarter
        w_ref[start : start + quarter, start : start + quarter] = corner
    ri = lax.broadcasted_iota(jnp.int32, (n, n), 0)
    ci = lax.broadcasted_iota(jnp.int32, (n, n), 1)
    w_ref[:, n:] = jnp.where(ri == ci, 1.0, 0.0)
    full=(SUB,LANE)
    sub=lax.broadcasted_iota(jnp.int32,full,0)
    lane=lax.broadcasted_iota(jnp.int32,full,1)
    zero=jnp.zeros(full,jnp.float32)
    def span(k): return (k//LANE)*LANE, n+((k+SUB+LANE-1)//LANE)*LANE
    def lanebc(x,o): return jnp.broadcast_to(x[:,o:o+1],full)
    def subbc(x,i): return jnp.broadcast_to(x[i:i+1,:],full)
    def load(k):
        lo,hi=span(k)
        P={t: w_ref[k:k+SUB,t*LANE:(t+1)*LANE] for t in range(lo//LANE,hi//LANE)}
        diag={}
        for j in range(SUB):
            c=lanebc(P[lo//LANE],k-lo+j)
            for i in range(j+1): diag[i,j]=subbc(c,i)
        return P,diag
    def loadp(k):
        lo,hi=span(k)
        return {t: w_ref[k:k+SUB,t*LANE:(t+1)*LANE] for t in range(lo//LANE,hi//LANE)}
    def diagof(P,k):
        diag={}
        for j in range(SUB):
            c=lanebc(P[k//LANE],k%LANE+j)
            for i in range(j+1): diag[i,j]=subbc(c,i)
        return diag
    def split3(x):
        h=x.astype(jnp.bfloat16); x=x-h.astype(jnp.float32)
        m=x.astype(jnp.bfloat16); x=x-m.astype(jnp.float32)
        return h,m,x.astype(jnp.bfloat16)
    coming={k: loadp(k) for k in range(0,min(DEPTH*SUB,n),SUB)}
    diag=diagof(coming[0],0)
    for k in range(0,n,SUB):
        lo,hi=span(k)
        tiles=range(lo//LANE,hi//LANE)
        nxt=k+SUB
        P=coming.pop(k)
        if nxt<n: ndiag=diagof(coming[nxt],nxt) if DEPTH>1 else None
        roots=zero
        for i in range(SUB):
            r=lax.rsqrt(diag[i,i])
            roots=jnp.where(sub==i,r,roots)
            if i<SUB-1:
                col=zero
                for j in range(i+1,SUB): col=jnp.where(sub==j,diag[i,j],col)
                col=col*(r*r)
                s={j: diag[i,j]*r for j in range(i+1,SUB)}
                for j in range(i+1,SUB):
                    for l in range(j,SUB): diag[j,l]=diag[j,l]-s[j]*s[l]
                for t in tiles: P[t]=P[t]-col*subbc(P[t],i)
        t0=lo//LANE
        done={t: P[t]*roots for t in tiles}
        done[t0]=jnp.where(lane>=(k-lo)+sub,done[t0],0.0)
        far=k+DEPTH*SUB
        if far<n: coming[far]=loadp(far)
        if nxt<n:
            tn,on=nxt//LANE,nxt%LANE
            E=[lanebc(done[tn],on+j) for j in range(SUB)]
            for i in range(SUB):
                for j in range(i,SUB):
                    ndiag[i,j]=ndiag[i,j]-jnp.broadcast_to(jnp.sum(E[i]*E[j],axis=0,keepdims=True),full)
            for kk in range(SUB):
                row={t: subbc(done[t],kk) for t in done}
                for q in coming:
                    tq,oq=q//LANE,q%LANE
                    c=jnp.sum(jnp.where(lane==oq+sub,row[tq],0.0),axis=1,keepdims=True)
                    c=jnp.broadcast_to(c,full)
                    for t in row:
                        if t in coming[q]: coming[q][t]=coming[q][t]-c*row[t]
        U=jnp.concatenate([done[t] for t in tiles],axis=1)
        if lo: u_ref[k:k+SUB,:lo]=jnp.zeros((SUB,lo),jnp.float32)
        u_ref[k:k+SUB,lo:]=U[:,:n-lo]
        v_ref[k:k+SUB,:hi-n]=U[:,n-lo:]
        if hi<2*n: v_ref[k:k+SUB,hi-n:]=jnp.zeros((SUB,2*n-hi),jnp.float32)
        below=far+SUB
        if below<n:
            lane1=(below//LANE)*LANE
            h,m,l=split3(U[:,lane1-lo:])
            lhs=jnp.concatenate([x[:,:n-lane1].astype(jnp.float32) for x in (h,h,m,h,l,m)],axis=0).astype(jnp.bfloat16)
            rhs=jnp.concatenate([x.astype(jnp.float32) for x in (h,m,h,l,h,m)],axis=0).astype(jnp.bfloat16)
            M=lax.dot_general(lhs,rhs,(((0,),(0,)),((),())),preferred_element_type=jnp.float32)
            w_ref[below:, lane1:hi]=w_ref[below:, lane1:hi]-M[below-lane1:,:]
        if nxt<n: diag=ndiag


def factored(place, own, other, scale):
    n = own.shape[-1] * 2
    return pl.pallas_call(
        functools.partial(factor_kernel, scale),
        in_specs=[SCALARS, WHOLE, WHOLE],
        out_specs=(WHOLE, WHOLE),
        out_shape=(floats(n, n), floats(n, n)),
        scratch_shapes=[pltpu.VMEM((n, 2 * n), jnp.float32)],
        compiler_params=LIMIT,
        name="factor",
    )(place, own, other)


def turn_kernel(factor_ref, *refs):
    factor = split(factor_ref[...])
    out_ref = refs[-1]
    for which, slab_ref in enumerate(refs[:-1]):
        for a in range(slab_ref.shape[0]):
            turned = product(factor, split(slab_ref[a]), ((1,), (0,)))
            out_ref[:, which, a] = turned.reshape(
                out_ref.shape[0], out_ref.shape[3], out_ref.shape[4]
            )


def turned_by(factor, slabs, dests):
    depth, n, _ = slabs[0].shape
    cols = factor.shape[0] // dests
    if cols % SUB:
        stacked = jnp.stack(slabs)
        moved = jnp.einsum("djb,sabk->dsajk", factor.reshape(dests, cols, n), stacked, precision=FAST)
        return moved
    step = max(1, 4 // len(slabs))
    step = step if depth % step == 0 else 1
    return pl.pallas_call(
        turn_kernel,
        grid=(depth // step,),
        in_specs=[pl.BlockSpec(factor.shape, lambda g: (0, 0))]
        + [pl.BlockSpec((step, n, n), lambda g: (g, 0, 0))] * len(slabs),
        out_specs=pl.BlockSpec((dests, len(slabs), step, cols, n), lambda g: (0, 0, g, 0, 0)),
        out_shape=pltpu.HBM((dests, len(slabs), depth, cols, n), jnp.float32),
        compiler_params=LIMIT,
        name="turn",
    )(factor, *map(in_hbm, slabs))


def move_kernel(place_ref, factor_ref, x_ref, y_ref, *refs):
    moved_refs, (kept_ref, sent_ref, terms_ref) = refs[:-3], refs[-3:]
    step = pl.program_id(0)

    @pl.when(step == 0)
    def _():
        terms_ref[...] = jnp.zeros_like(terms_ref)

    factor = split(factor_ref[...])
    depth, cols, lanes = x_ref.shape
    flat = [ref.reshape(depth * cols, lanes) for ref in (x_ref, y_ref)]
    terms = terms_ref[...]
    for s in range(cols):
        parts = [ref[pl.ds(s, depth, stride=cols), :] for ref in flat]
        moved = product(factor, split(jnp.concatenate(parts, axis=1)), ((1,), (0,)))
        rows = depth // len(moved_refs)
        for which, ref in enumerate(moved_refs):
            ref[s] = moved[which * rows : (which + 1) * rows]
        terms = terms + gram_terms(moved)
    terms_ref[...] = terms

    @pl.when(step == pl.num_programs(0) - 1)
    def _():
        put_parts(gram_of(terms), place_ref[0], kept_ref, sent_ref)


def moved_by(place, factor, gathered, outputs):
    depth, cols, n = gathered.shape
    part = packed_shape(n)
    if cols % SUB:
        moved = jnp.einsum("ia,ajk->jik", factor, gathered, precision=FAST)
        flat = moved.reshape(-1, n)
        gram = jnp.einsum("rc,rd->cd", flat, flat, precision=lax.Precision.HIGHEST)
        parts = packed(gram, 0), packed(gram, 1)
        first = place[0] == 0
        kept, sent = jnp.where(first, *parts), jnp.where(first, *parts[::-1])
        return (*jnp.split(moved, outputs, axis=1), kept, sent)
    rows = depth // outputs
    return pl.pallas_call(
        move_kernel,
        grid=(cols // SUB,),
        in_specs=[
            SCALARS,
            pl.BlockSpec(factor.shape, lambda g: (0, 0)),
            pl.BlockSpec((depth, SUB, n // 2), lambda g: (0, g, 0)),
            pl.BlockSpec((depth, SUB, n // 2), lambda g: (0, g, 1)),
        ],
        out_specs=[pl.BlockSpec((SUB, rows, n), lambda g: (g, 0, 0))] * outputs
        + [pl.BlockSpec(part.shape, lambda g: (0, 0))] * 2,
        out_shape=[pltpu.HBM((cols, rows, n), jnp.float32)] * outputs + [part, part],
        scratch_shapes=[pltpu.VMEM((n, 2 * n), jnp.float32)],
        compiler_params=LIMIT,
        name="move",
    )(place, factor, in_hbm(gathered), in_hbm(gathered))


def base_kernel(inverse_ref, moved_ref, out_ref):
    inverse = split(inverse_ref[...])
    cols, rows, _ = moved_ref.shape
    flat = out_ref.reshape(rows * cols, out_ref.shape[2])
    for s in range(cols):
        flat[pl.ds(s, rows, stride=cols), :] = product(split(moved_ref[s]), inverse, ((1,), (1,)))


def bases_of(inverse, moved):
    cols, rows, n = moved.shape
    if cols % SUB:
        return jnp.einsum("jik,lk->ijl", moved, inverse, precision=FAST)
    return pl.pallas_call(
        base_kernel,
        grid=(cols // SUB, 2),
        in_specs=[
            pl.BlockSpec((n // 2, n), lambda g, h: (h, 0)),
            pl.BlockSpec((SUB, rows, n), lambda g, h: (g, 0, 0)),
        ],
        out_specs=pl.BlockSpec((rows, SUB, n // 2), lambda g, h: (0, g, h)),
        out_shape=floats(rows, cols, n),
        compiler_params=LIMIT,
        name="bases",
    )(inverse, in_hbm(moved))


def masks_of():
    masks = [1]
    while 2 * masks[-1] < lax.axis_size("row"):
        masks.append(2 * masks[-1])
    return masks


def first_round(kept, sent):
    return kept + swapped(sent, "row", 1)


def later_rounds(total):
    for mask in masks_of()[1:]:
        total = total + swapped(total, "row", mask)
    return total


def tied(one, other):
    return lax.optimization_barrier((one, other))


def sorted_by(factor, rows_from, cols_from):
    n = factor.shape[0]
    ids = jnp.arange(n, dtype=jnp.int32)
    high = lax.Precision.HIGHEST
    chosen = (ids[:, None] == cols_from[None, :]).astype(jnp.float32)
    factor = jnp.dot(factor, chosen, precision=high)
    chosen = (rows_from[:, None] == ids[None, :]).astype(jnp.float32)
    return jnp.dot(chosen, factor, precision=high)


def body(leaves, level_one, level_two):
    rows = lax.axis_size("row")
    rank = leaves.shape[-1]
    node = lax.axis_index("node") % 2
    is_left = node == 0
    place = jnp.stack([lax.axis_index("row") % 2]).astype(jnp.int32)

    def factors_of(part, scale):
        return factored(place, part, swapped(part, "row", 1), scale)

    own_two = level_two[0]
    sibling_two = swapped(own_two, "node", 1)

    leaf_scale = 1.0 / (leaves.shape[1] * rows)
    masks = masks_of()
    right_part = first_round(*leaf_partial(place, leaves, 1))
    left_part, left_sent = leaf_partial(place, leaves, 0)
    rounds = [lambda part: part + swapped(left_sent, "row", 1)]
    for mask in masks[1:]:
        rounds.append(lambda part, mask=mask: part + swapped(part, "row", mask))
    for index, mask in enumerate(masks[1:], 1):
        if index >= 2:
            right_part, left_part = tied(right_part, left_part)
            left_part = rounds[index - 2](left_part)
        right_part = right_part + swapped(right_part, "row", mask)
    right_part, left_part = tied(right_part, left_part)
    left_part = rounds[-2](left_part)
    right_upper, right_inverse = factors_of(right_part, leaf_scale)
    right_upper, left_part = tied(right_upper, left_part)
    left_part = rounds[-1](left_part)
    turned = turned_by(right_upper, [level_one[0]], rows)
    turned, left_part = tied(turned, left_part)
    gathered = lax.all_to_all(turned, "row", 0, 0, tiled=True)

    left_upper, left_inverse = factors_of(left_part, leaf_scale)
    leaf_bases = leaf_bases_of(leaves, left_inverse, right_inverse)
    gathered, leaf_bases = lax.optimization_barrier((gathered, leaf_bases))

    cols = gathered.shape[3]
    moved_one, kept, sent = moved_by(place, left_upper, gathered.reshape(rank, cols, rank), 1)
    own_part = later_rounds(first_round(kept, sent))
    sibling_part = swapped(own_part, "node", 1)
    scale = 1.0 / (rank * rank)
    right_upper, right_inverse = factors_of(jnp.where(is_left, sibling_part, own_part), scale)

    chosen = right_upper.reshape(rows, 2, -1, rank).transpose(1, 0, 2, 3)
    chosen = lax.dynamic_index_in_dim(chosen, node, 0, keepdims=False).reshape(-1, rank)
    turned = turned_by(chosen, [own_two, sibling_two], rows)
    gathered = lax.all_to_all(turned, "row", 0, 0, tiled=True)

    left_upper, left_inverse = factors_of(jnp.where(is_left, own_part, sibling_part), scale)
    one_inverse = jnp.where(is_left, left_inverse, right_inverse)
    level_one_bases = bases_of(one_inverse, moved_one)[None]
    ids = jnp.arange(rank, dtype=jnp.int32)
    depth = own_two.shape[0]
    rows_from = 2 * (ids % (rank // 2)) + (ids // (rank // 2) + node) % 2
    cols_from = ids // (2 * depth) * (2 * depth) + 2 * (ids % depth) + (ids // depth + node) % 2
    sorted_left = sorted_by(left_upper, rows_from, cols_from)
    gathered, level_one_bases, sorted_left = lax.optimization_barrier(
        (gathered, level_one_bases, sorted_left)
    )

    cols = gathered.shape[3]
    mine, theirs, kept, sent = moved_by(place, sorted_left, gathered.reshape(rank, cols, rank), 2)
    part = first_round(kept, sent)
    part = part + swapped(part, "node", 1)
    theirs, part = tied(theirs, part)
    received = swapped(theirs, "node", 1)
    two_upper, two_inverse = factors_of(later_rounds(part), scale)
    whole_two = jnp.where(
        is_left, jnp.concatenate([mine, received]), jnp.concatenate([received, mine])
    )
    level_two_bases = bases_of(two_inverse, whole_two)[None]
    return (leaf_bases, level_one_bases, level_two_bases, two_upper[None])


def solution(mesh):
    placed = (P("node", "row", None), P("node", "row", None, None), P("node", "row", None, None))
    return jax.shard_map(
        body,
        mesh=mesh,
        in_specs=placed,
        out_specs=(
            P("node", "row", None),
            P("node", None, "row", None),
            P("node", None, "row", None),
            P("node", None, None),
        ),
        check_vma=False,
    )
```

```python
import functools
import jax
import jax.numpy as jnp
from jax import lax
from jax.experimental import pallas as pl
from jax.experimental.pallas import tpu as pltpu
from jax.sharding import PartitionSpec as P

FAST = lax.Precision.HIGH
SUB = 8
LANE = 128
DEPTH = 2
WHOLE = pl.BlockSpec(memory_space=pltpu.VMEM)
SCALARS = pl.BlockSpec(memory_space=pltpu.SMEM)
LIMIT = pltpu.CompilerParams(vmem_limit_bytes=48 * 2**20)


def in_hbm(value):
    return pltpu.with_memory_space_constraint(value, pltpu.HBM)


def floats(*shape):
    return jax.ShapeDtypeStruct(shape, jnp.float32)


def swapped(value, axis, mask):
    pairs = [(source, source ^ mask) for source in range(lax.axis_size(axis))]
    return lax.ppermute(value, axis, pairs)


def split(value):
    high = value.astype(jnp.bfloat16)
    return high, (value - high.astype(jnp.float32)).astype(jnp.bfloat16)


def product(left, right, dims):
    def dot(one, other):
        return lax.dot_general(one, other, (dims, ((), ())), preferred_element_type=jnp.float32)

    if dims[0] == (1,):
        rows = left[0].shape[0]
        both = dot(jnp.concatenate(left, axis=0), right[0])
        return both[:rows] + (dot(left[0], right[1]) + both[rows:])
    return dot(left[0], right[0]) + (dot(left[0], right[1]) + dot(left[1], right[0]))


def gram_terms(value):
    high, low = split(value)
    both = jnp.concatenate([high, low], axis=1)
    return lax.dot_general(
        high, both, (((0,), (0,)), ((), ())), preferred_element_type=jnp.float32
    )


def gram_of(terms):
    n = terms.shape[0]
    return terms[:, :n] + (terms[:, n:] + terms[:, n:].T)


def packed(gram, core):
    half, quarter = gram.shape[0] // 2, gram.shape[0] // 4
    if core == 0:
        square, row, corner = gram[:quarter, :half], gram[:quarter, half:], gram[-quarter:, -quarter:]
    else:
        square, row = gram[half : half + quarter, half:], gram[quarter:half, half:]
        corner = gram[quarter:half, quarter:half]
    corner = jnp.concatenate([corner[: quarter // 2], corner[quarter // 2 :]], axis=1)
    return jnp.concatenate([square, row, corner], axis=0)


def packed_shape(n):
    return floats(n // 4 * 2 + n // 8, n // 2)


def put_parts(gram, core, kept_ref, sent_ref):
    first, second = packed(gram, 0), packed(gram, 1)
    kept_ref[...] = jnp.where(core == 0, first, second)
    sent_ref[...] = jnp.where(core == 0, second, first)


def leaf_kernel(place_ref, leaf_ref, kept_ref, sent_ref):
    _, rows, n = leaf_ref.shape
    step = min(rows, 256)
    terms = jnp.zeros((n, 2 * n), jnp.float32)
    for start in range(0, rows, step):
        terms = terms + gram_terms(leaf_ref[0, start : start + step, :])
    put_parts(gram_of(terms), place_ref[0], kept_ref, sent_ref)


def leaf_partial(place, leaves, leaf):
    _, rows, n = leaves.shape
    part = packed_shape(n)
    return pl.pallas_call(
        leaf_kernel,
        grid=(1,),
        in_specs=[SCALARS, pl.BlockSpec((1, rows, n), lambda g: (leaf, 0, 0))],
        out_specs=(pl.BlockSpec(part.shape, lambda g: (0, 0)),) * 2,
        out_shape=(part, part),
        compiler_params=LIMIT,
        name="leaf_partial",
    )(place, in_hbm(leaves))


def leaf_base_kernel(leaf_ref, first_ref, second_ref, out_ref):
    for leaf, ref in enumerate((first_ref, second_ref)):
        inverse = split(ref[...])
        out_ref[leaf] = product(split(leaf_ref[leaf]), inverse, ((1,), (1,)))


def leaf_bases_of(leaves, first, second):
    count, rows, n = leaves.shape
    step = min(rows, 256)
    return pl.pallas_call(
        leaf_base_kernel,
        grid=(rows // step,),
        in_specs=[pl.BlockSpec((count, step, n), lambda g: (0, g, 0))]
        + [pl.BlockSpec((n, n), lambda g: (0, 0))] * 2,
        out_specs=pl.BlockSpec((count, step, n), lambda g: (0, g, 0)),
        out_shape=floats(count, rows, n),
        compiler_params=LIMIT,
        name="leaf_bases",
    )(in_hbm(leaves), first, second)


def factor_kernel(scale, place_ref, own_ref, other_ref, u_ref, v_ref, w_ref):
    n = u_ref.shape[0]
    half, quarter = n // 2, n // 4
    own, other = own_ref[...] * scale, other_ref[...] * scale
    mine = place_ref[0] == 0
    w_ref[:, :n] = jnp.zeros((n, n), jnp.float32)
    for core, part in ((0, jnp.where(mine, own, other)), (1, jnp.where(mine, other, own))):
        square, row, corner = part[:quarter], part[quarter:half], part[half:]
        corner = jnp.concatenate([corner[:, :quarter], corner[:, quarter:]], axis=0)
        start = core * half
        w_ref[start : start + quarter, start : start + half] = square
        w_ref[core * quarter : (core + 1) * quarter, half:n] = row
        start = n - quarter if core == 0 else quarter
        w_ref[start : start + quarter, start : start + quarter] = corner
    ri = lax.broadcasted_iota(jnp.int32, (n, n), 0)
    ci = lax.broadcasted_iota(jnp.int32, (n, n), 1)
    w_ref[:, n:] = jnp.where(ri == ci, 1.0, 0.0)
    full=(SUB,LANE)
    sub=lax.broadcasted_iota(jnp.int32,full,0)
    lane=lax.broadcasted_iota(jnp.int32,full,1)
    zero=jnp.zeros(full,jnp.float32)
    def span(k): return (k//LANE)*LANE, n+((k+SUB+LANE-1)//LANE)*LANE
    def lanebc(x,o): return jnp.broadcast_to(x[:,o:o+1],full)
    def subbc(x,i): return jnp.broadcast_to(x[i:i+1,:],full)
    def load(k):
        lo,hi=span(k)
        P={t: w_ref[k:k+SUB,t*LANE:(t+1)*LANE] for t in range(lo//LANE,hi//LANE)}
        diag={}
        for j in range(SUB):
            c=lanebc(P[lo//LANE],k-lo+j)
            for i in range(j+1): diag[i,j]=subbc(c,i)
        return P,diag
    def loadp(k):
        lo,hi=span(k)
        return {t: w_ref[k:k+SUB,t*LANE:(t+1)*LANE] for t in range(lo//LANE,hi//LANE)}
    def diagof(P,k):
        diag={}
        for j in range(SUB):
            c=lanebc(P[k//LANE],k%LANE+j)
            for i in range(j+1): diag[i,j]=subbc(c,i)
        return diag
    def split3(x):
        h=x.astype(jnp.bfloat16); x=x-h.astype(jnp.float32)
        m=x.astype(jnp.bfloat16); x=x-m.astype(jnp.float32)
        return h,m,x.astype(jnp.bfloat16)
    coming={k: loadp(k) for k in range(0,min(DEPTH*SUB,n),SUB)}
    diag=diagof(coming[0],0)
    for k in range(0,n,SUB):
        lo,hi=span(k)
        tiles=range(lo//LANE,hi//LANE)
        nxt=k+SUB
        P=coming.pop(k)
        if nxt<n: ndiag=diagof(coming[nxt],nxt) if DEPTH>1 else None
        roots=zero
        for i in range(SUB):
            r=lax.rsqrt(diag[i,i])
            roots=jnp.where(sub==i,r,roots)
            if i<SUB-1:
                col=zero
                for j in range(i+1,SUB): col=jnp.where(sub==j,diag[i,j],col)
                col=col*(r*r)
                s={j: diag[i,j]*r for j in range(i+1,SUB)}
                for j in range(i+1,SUB):
                    for l in range(j,SUB): diag[j,l]=diag[j,l]-s[j]*s[l]
                for t in tiles: P[t]=P[t]-col*subbc(P[t],i)
        t0=lo//LANE
        done={t: P[t]*roots for t in tiles}
        done[t0]=jnp.where(lane>=(k-lo)+sub,done[t0],0.0)
        far=k+DEPTH*SUB
        if far<n: coming[far]=loadp(far)
        if nxt<n:
            tn,on=nxt//LANE,nxt%LANE
            E=[lanebc(done[tn],on+j) for j in range(SUB)]
            for i in range(SUB):
                for j in range(i,SUB):
                    ndiag[i,j]=ndiag[i,j]-jnp.broadcast_to(jnp.sum(E[i]*E[j],axis=0,keepdims=True),full)
            for kk in range(SUB):
                row={t: subbc(done[t],kk) for t in done}
                for q in coming:
                    tq,oq=q//LANE,q%LANE
                    c=jnp.sum(jnp.where(lane==oq+sub,row[tq],0.0),axis=1,keepdims=True)
                    c=jnp.broadcast_to(c,full)
                    for t in row:
                        if t in coming[q]: coming[q][t]=coming[q][t]-c*row[t]
        U=jnp.concatenate([done[t] for t in tiles],axis=1)
        if lo: u_ref[k:k+SUB,:lo]=jnp.zeros((SUB,lo),jnp.float32)
        u_ref[k:k+SUB,lo:]=U[:,:n-lo]
        v_ref[k:k+SUB,:hi-n]=U[:,n-lo:]
        if hi<2*n: v_ref[k:k+SUB,hi-n:]=jnp.zeros((SUB,2*n-hi),jnp.float32)
        below=far+SUB
        if below<n:
            lane1=(below//LANE)*LANE
            h,m,l=split3(U[:,lane1-lo:])
            lhs=jnp.concatenate([x[:,:n-lane1].astype(jnp.float32) for x in (h,h,m,h,l,m)],axis=0).astype(jnp.bfloat16)
            rhs=jnp.concatenate([x.astype(jnp.float32) for x in (h,m,h,l,h,m)],axis=0).astype(jnp.bfloat16)
            M=lax.dot_general(lhs,rhs,(((0,),(0,)),((),())),preferred_element_type=jnp.float32)
            w_ref[below:, lane1:hi]=w_ref[below:, lane1:hi]-M[below-lane1:,:]
        if nxt<n: diag=ndiag


def factored(place, own, other, scale):
    n = own.shape[-1] * 2
    return pl.pallas_call(
        functools.partial(factor_kernel, scale),
        in_specs=[SCALARS, WHOLE, WHOLE],
        out_specs=(WHOLE, WHOLE),
        out_shape=(floats(n, n), floats(n, n)),
        scratch_shapes=[pltpu.VMEM((n, 2 * n), jnp.float32)],
        compiler_params=LIMIT,
        name="factor",
    )(place, own, other)


def terms_kernel(*refs):
    count = len(refs) // 3
    for which in range(count):
        high, low = split(refs[which][...])
        refs[count + 2 * which][...] = high
        refs[count + 2 * which + 1][...] = low


def terms_of(slabs):
    depth, n, _ = slabs[0].shape
    step = 2 if depth % 2 == 0 else 1
    block = pl.BlockSpec((step, n, n), lambda g: (g, 0, 0))
    outs = pl.pallas_call(
        terms_kernel,
        grid=(depth // step,),
        in_specs=[block] * len(slabs),
        out_specs=[block] * (2 * len(slabs)),
        out_shape=[jax.ShapeDtypeStruct((depth, n, n), jnp.bfloat16)] * (2 * len(slabs)),
        compiler_params=LIMIT,
        name="terms",
    )(*slabs)
    return [tuple(outs[2 * which : 2 * which + 2]) for which in range(len(slabs))]


def turn_kernel(factor_ref, *refs):
    factor = split(factor_ref[...])
    out_ref = refs[-1]
    for which in range(len(refs) // 2):
        high_ref, low_ref = refs[2 * which : 2 * which + 2]
        for a in range(high_ref.shape[0]):
            turned = product(factor, (high_ref[a], low_ref[a]), ((1,), (0,)))
            out_ref[:, which, a] = turned.reshape(
                out_ref.shape[0], out_ref.shape[3], out_ref.shape[4]
            )


def turned_by(factor, slabs, dests):
    depth, n, _ = slabs[0][0].shape
    cols = factor.shape[0] // dests
    if cols % SUB:
        wide = [high.astype(jnp.float32) + low.astype(jnp.float32) for high, low in slabs]
        rows = factor.reshape(dests, cols, n)
        return jnp.einsum("djb,sabk->dsajk", rows, jnp.stack(wide), precision=FAST)
    step = max(1, 4 // len(slabs))
    step = step if depth % step == 0 else 1
    return pl.pallas_call(
        turn_kernel,
        grid=(depth // step,),
        in_specs=[pl.BlockSpec(factor.shape, lambda g: (0, 0))]
        + [pl.BlockSpec((step, n, n), lambda g: (g, 0, 0))] * (2 * len(slabs)),
        out_specs=pl.BlockSpec((dests, len(slabs), step, cols, n), lambda g: (0, 0, g, 0, 0)),
        out_shape=pltpu.HBM((dests, len(slabs), depth, cols, n), jnp.float32),
        compiler_params=LIMIT,
        name="turn",
    )(factor, *[term for slab in slabs for term in slab])


def move_kernel(place_ref, factor_ref, x_ref, y_ref, *refs):
    moved_refs, (kept_ref, sent_ref, terms_ref) = refs[:-3], refs[-3:]
    step = pl.program_id(0)

    @pl.when(step == 0)
    def _():
        terms_ref[...] = jnp.zeros_like(terms_ref)

    factor = split(factor_ref[...])
    depth, cols, lanes = x_ref.shape
    flat = [ref.reshape(depth * cols, lanes) for ref in (x_ref, y_ref)]
    terms = terms_ref[...]
    for s in range(cols):
        parts = [ref[pl.ds(s, depth, stride=cols), :] for ref in flat]
        moved = product(factor, split(jnp.concatenate(parts, axis=1)), ((1,), (0,)))
        rows = depth // len(moved_refs)
        for which, ref in enumerate(moved_refs):
            ref[s] = moved[which * rows : (which + 1) * rows]
        terms = terms + gram_terms(moved)
    terms_ref[...] = terms

    @pl.when(step == pl.num_programs(0) - 1)
    def _():
        put_parts(gram_of(terms), place_ref[0], kept_ref, sent_ref)


def moved_by(place, factor, gathered, outputs):
    depth, cols, n = gathered.shape
    part = packed_shape(n)
    if cols % SUB:
        moved = jnp.einsum("ia,ajk->jik", factor, gathered, precision=FAST)
        flat = moved.reshape(-1, n)
        gram = jnp.einsum("rc,rd->cd", flat, flat, precision=lax.Precision.HIGHEST)
        parts = packed(gram, 0), packed(gram, 1)
        first = place[0] == 0
        kept, sent = jnp.where(first, *parts), jnp.where(first, *parts[::-1])
        return (*jnp.split(moved, outputs, axis=1), kept, sent)
    rows = depth // outputs
    return pl.pallas_call(
        move_kernel,
        grid=(cols // SUB,),
        in_specs=[
            SCALARS,
            pl.BlockSpec(factor.shape, lambda g: (0, 0)),
            pl.BlockSpec((depth, SUB, n // 2), lambda g: (0, g, 0)),
            pl.BlockSpec((depth, SUB, n // 2), lambda g: (0, g, 1)),
        ],
        out_specs=[pl.BlockSpec((SUB, rows, n), lambda g: (g, 0, 0))] * outputs
        + [pl.BlockSpec(part.shape, lambda g: (0, 0))] * 2,
        out_shape=[pltpu.HBM((cols, rows, n), jnp.float32)] * outputs + [part, part],
        scratch_shapes=[pltpu.VMEM((n, 2 * n), jnp.float32)],
        compiler_params=LIMIT,
        name="move",
    )(place, factor, gathered, gathered)


def base_kernel(inverse_ref, moved_ref, out_ref):
    inverse = split(inverse_ref[...])
    cols, rows, _ = moved_ref.shape
    flat = out_ref.reshape(rows * cols, out_ref.shape[2])
    for s in range(cols):
        flat[pl.ds(s, rows, stride=cols), :] = product(split(moved_ref[s]), inverse, ((1,), (1,)))


def bases_of(inverse, moved):
    cols, rows, n = moved.shape
    if cols % SUB:
        return jnp.einsum("jik,lk->ijl", moved, inverse, precision=FAST)
    return pl.pallas_call(
        base_kernel,
        grid=(cols // SUB, 2),
        in_specs=[
            pl.BlockSpec((n // 2, n), lambda g, h: (h, 0)),
            pl.BlockSpec((SUB, rows, n), lambda g, h: (g, 0, 0)),
        ],
        out_specs=pl.BlockSpec((rows, SUB, n // 2), lambda g, h: (0, g, h)),
        out_shape=floats(rows, cols, n),
        compiler_params=LIMIT,
        name="bases",
    )(inverse, moved)


def joined_kernel(node_ref, inverse_ref, mine_ref, other_ref, out_ref):
    inverse = split(inverse_ref[...])
    cols, rows, _ = mine_ref.shape
    flat = out_ref.reshape(rows * cols, out_ref.shape[2])
    own = pl.program_id(0) == node_ref[0]
    for s in range(cols):
        moved = jnp.where(own, mine_ref[s], other_ref[s])
        flat[pl.ds(s, rows, stride=cols), :] = product(split(moved), inverse, ((1,), (1,)))


def joined_bases(node, inverse, mine, other):
    cols, rows, n = mine.shape
    if cols % SUB:
        left = node[0] == 0
        first, second = jnp.where(left, mine, other), jnp.where(left, other, mine)
        return bases_of(inverse, jnp.concatenate([first, second]))
    return pl.pallas_call(
        joined_kernel,
        grid=(2, 2),
        in_specs=[SCALARS, pl.BlockSpec((n // 2, n), lambda g, h: (h, 0))]
        + [pl.BlockSpec((cols, rows, n), lambda g, h: (0, 0, 0))] * 2,
        out_specs=pl.BlockSpec((rows, cols, n // 2), lambda g, h: (0, g, h)),
        out_shape=floats(rows, 2 * cols, n),
        compiler_params=LIMIT,
        name="joined_bases",
    )(node, inverse, mine, other)


def masks_of():
    masks = [1]
    while 2 * masks[-1] < lax.axis_size("row"):
        masks.append(2 * masks[-1])
    return masks


def first_round(kept, sent):
    return kept + swapped(sent, "row", 1)


def later_rounds(total):
    for mask in masks_of()[1:]:
        total = total + swapped(total, "row", mask)
    return total


def tied(one, other):
    return lax.optimization_barrier((one, other))


def sorted_by(factor, rows_from, cols_from):
    n = factor.shape[0]
    ids = jnp.arange(n, dtype=jnp.int32)
    high = lax.Precision.HIGHEST
    chosen = (ids[:, None] == cols_from[None, :]).astype(jnp.float32)
    factor = jnp.dot(factor, chosen, precision=high)
    chosen = (rows_from[:, None] == ids[None, :]).astype(jnp.float32)
    return jnp.dot(chosen, factor, precision=high)


def body(leaves, level_one, level_two):
    rows = lax.axis_size("row")
    rank = leaves.shape[-1]
    node = lax.axis_index("node") % 2
    is_left = node == 0
    place = jnp.stack([lax.axis_index("row") % 2]).astype(jnp.int32)

    def factors_of(part, scale):
        return factored(place, part, swapped(part, "row", 1), scale)

    own_two = level_two[0]
    sibling_two = swapped(own_two, "node", 1)

    leaf_scale = 1.0 / (leaves.shape[1] * rows)
    masks = masks_of()
    right_part = first_round(*leaf_partial(place, leaves, 1))
    left_part, left_sent = leaf_partial(place, leaves, 0)
    rounds = [lambda part: part + swapped(left_sent, "row", 1)]
    for mask in masks[1:]:
        rounds.append(lambda part, mask=mask: part + swapped(part, "row", mask))
    slab, right_part = tied(level_one[0], right_part)
    (slab,) = terms_of([in_hbm(slab)])
    for index, mask in enumerate(masks[1:], 1):
        if index == len(masks) - 2:
            right_part, slab, left_part = lax.optimization_barrier((right_part, slab, left_part))
        if index >= len(masks) - 2:
            right_part, left_part = tied(right_part, left_part)
            left_part = rounds[index - len(masks) + 2](left_part)
        right_part = right_part + swapped(right_part, "row", mask)
    right_part, left_part = tied(right_part, left_part)
    right_upper, right_inverse = factors_of(right_part, leaf_scale)
    right_upper, left_part = tied(right_upper, left_part)
    left_part = rounds[2](left_part)
    turned = turned_by(right_upper, [slab], rows)
    gathered = lax.all_to_all(turned, "row", 0, 0, tiled=True)
    for later in rounds[3:]:
        left_part = later(left_part)

    left_upper, left_inverse = factors_of(left_part, leaf_scale)
    leaf_bases = leaf_bases_of(leaves, left_inverse, right_inverse)
    gathered, leaf_bases = lax.optimization_barrier((gathered, leaf_bases))

    cols = gathered.shape[3]
    moved_one, kept, sent = moved_by(place, left_upper, gathered.reshape(rank, cols, rank), 1)
    part = first_round(kept, sent)
    part, own_two, sibling_two = lax.optimization_barrier((part, own_two, sibling_two))
    slabs = terms_of([own_two, sibling_two])
    own_part, slabs = tied(later_rounds(part), slabs)
    sibling_part = swapped(own_part, "node", 1)
    scale = 1.0 / (rank * rank)
    right_upper, right_inverse = factors_of(jnp.where(is_left, sibling_part, own_part), scale)

    chosen = right_upper.reshape(rows, 2, -1, rank).transpose(1, 0, 2, 3)
    chosen = lax.dynamic_index_in_dim(chosen, node, 0, keepdims=False).reshape(-1, rank)
    turned = turned_by(chosen, slabs, rows)
    gathered = lax.all_to_all(turned, "row", 0, 0, tiled=True)

    left_upper, left_inverse = factors_of(jnp.where(is_left, own_part, sibling_part), scale)
    one_inverse = jnp.where(is_left, left_inverse, right_inverse)
    level_one_bases = bases_of(one_inverse, moved_one)[None]
    ids = jnp.arange(rank, dtype=jnp.int32)
    depth = own_two.shape[0]
    rows_from = 2 * (ids % (rank // 2)) + (ids // (rank // 2) + node) % 2
    cols_from = ids // (2 * depth) * (2 * depth) + 2 * (ids % depth) + (ids // depth + node) % 2
    sorted_left = sorted_by(left_upper, rows_from, cols_from)
    gathered, level_one_bases, sorted_left = lax.optimization_barrier(
        (gathered, level_one_bases, sorted_left)
    )

    cols = gathered.shape[3]
    mine, theirs, kept, sent = moved_by(place, sorted_left, gathered.reshape(rank, cols, rank), 2)
    part = first_round(kept, sent)
    part = part + swapped(part, "node", 1)
    theirs, part = tied(theirs, part)
    received = swapped(theirs, "node", 1)
    two_upper, two_inverse = factors_of(later_rounds(part), scale)
    place = jnp.stack([node]).astype(jnp.int32)
    level_two_bases = joined_bases(place, two_inverse, mine, received)[None]
    return (leaf_bases, level_one_bases, level_two_bases, two_upper[None])


def solution(mesh):
    placed = (P("node", "row", None), P("node", "row", None, None), P("node", "row", None, None))
    return jax.shard_map(
        body,
        mesh=mesh,
        in_specs=placed,
        out_specs=(
            P("node", "row", None),
            P("node", None, "row", None),
            P("node", None, "row", None),
            P("node", None, None),
        ),
        check_vma=False,
    )
```

```python
import functools
import jax
import jax.numpy as jnp
from jax import lax
from jax.experimental import pallas as pl
from jax.experimental.pallas import tpu as pltpu
from jax.sharding import PartitionSpec as P

FAST = lax.Precision.HIGH
SUB = 8
LANE = 128
DEPTH = 2
WHOLE = pl.BlockSpec(memory_space=pltpu.VMEM)
SCALARS = pl.BlockSpec(memory_space=pltpu.SMEM)
LIMIT = pltpu.CompilerParams(vmem_limit_bytes=48 * 2**20)


def in_hbm(value):
    return pltpu.with_memory_space_constraint(value, pltpu.HBM)


def floats(*shape):
    return jax.ShapeDtypeStruct(shape, jnp.float32)


def swapped(value, axis, mask):
    pairs = [(source, source ^ mask) for source in range(lax.axis_size(axis))]
    return lax.ppermute(value, axis, pairs)


def split(value):
    high = value.astype(jnp.bfloat16)
    return high, (value - high.astype(jnp.float32)).astype(jnp.bfloat16)


def product(left, right, dims):
    def dot(one, other):
        return lax.dot_general(one, other, (dims, ((), ())), preferred_element_type=jnp.float32)

    if dims[0] == (1,):
        rows = left[0].shape[0]
        both = dot(jnp.concatenate(left, axis=0), right[0])
        return both[:rows] + (dot(left[0], right[1]) + both[rows:])
    return dot(left[0], right[0]) + (dot(left[0], right[1]) + dot(left[1], right[0]))


def gram_terms(value):
    high, low = split(value)
    both = jnp.concatenate([high, low], axis=1)
    return lax.dot_general(
        high, both, (((0,), (0,)), ((), ())), preferred_element_type=jnp.float32
    )


def gram_of(terms):
    n = terms.shape[0]
    return terms[:, :n] + (terms[:, n:] + terms[:, n:].T)


def packed(gram, core):
    half, quarter = gram.shape[0] // 2, gram.shape[0] // 4
    if core == 0:
        square, row, corner = gram[:quarter, :half], gram[:quarter, half:], gram[-quarter:, -quarter:]
    else:
        square, row = gram[half : half + quarter, half:], gram[quarter:half, half:]
        corner = gram[quarter:half, quarter:half]
    corner = jnp.concatenate([corner[: quarter // 2], corner[quarter // 2 :]], axis=1)
    return jnp.concatenate([square, row, corner], axis=0)


def packed_shape(n):
    return floats(n // 4 * 2 + n // 8, n // 2)


def put_parts(gram, core, kept_ref, sent_ref):
    first, second = packed(gram, 0), packed(gram, 1)
    kept_ref[...] = jnp.where(core == 0, first, second)
    sent_ref[...] = jnp.where(core == 0, second, first)


def leaf_kernel(place_ref, leaf_ref, kept_ref, sent_ref):
    _, rows, n = leaf_ref.shape
    step = min(rows, 256)
    terms = jnp.zeros((n, 2 * n), jnp.float32)
    for start in range(0, rows, step):
        terms = terms + gram_terms(leaf_ref[0, start : start + step, :])
    put_parts(gram_of(terms), place_ref[0], kept_ref, sent_ref)


def leaf_partial(place, leaves, leaf):
    _, rows, n = leaves.shape
    part = packed_shape(n)
    return pl.pallas_call(
        leaf_kernel,
        grid=(1,),
        in_specs=[SCALARS, pl.BlockSpec((1, rows, n), lambda g: (leaf, 0, 0))],
        out_specs=(pl.BlockSpec(part.shape, lambda g: (0, 0)),) * 2,
        out_shape=(part, part),
        compiler_params=LIMIT,
        name="leaf_partial",
    )(place, in_hbm(leaves))


def leaf_base_kernel(leaf_ref, first_ref, second_ref, out_ref):
    for leaf, ref in enumerate((first_ref, second_ref)):
        inverse = split(ref[...])
        out_ref[leaf] = product(split(leaf_ref[leaf]), inverse, ((1,), (1,)))


def leaf_bases_of(leaves, first, second):
    count, rows, n = leaves.shape
    step = min(rows, 256)
    return pl.pallas_call(
        leaf_base_kernel,
        grid=(rows // step,),
        in_specs=[pl.BlockSpec((count, step, n), lambda g: (0, g, 0))]
        + [pl.BlockSpec((n, n), lambda g: (0, 0))] * 2,
        out_specs=pl.BlockSpec((count, step, n), lambda g: (0, g, 0)),
        out_shape=floats(count, rows, n),
        compiler_params=LIMIT,
        name="leaf_bases",
    )(in_hbm(leaves), first, second)


def factor_kernel(scale, place_ref, own_ref, other_ref, u_ref, v_ref, w_ref):
    n = u_ref.shape[0]
    half, quarter = n // 2, n // 4
    own, other = own_ref[...] * scale, other_ref[...] * scale
    mine = place_ref[0] == 0
    w_ref[:, :n] = jnp.zeros((n, n), jnp.float32)
    for core, part in ((0, jnp.where(mine, own, other)), (1, jnp.where(mine, other, own))):
        square, row, corner = part[:quarter], part[quarter:half], part[half:]
        corner = jnp.concatenate([corner[:, :quarter], corner[:, quarter:]], axis=0)
        start = core * half
        w_ref[start : start + quarter, start : start + half] = square
        w_ref[core * quarter : (core + 1) * quarter, half:n] = row
        start = n - quarter if core == 0 else quarter
        w_ref[start : start + quarter, start : start + quarter] = corner
    ri = lax.broadcasted_iota(jnp.int32, (n, n), 0)
    ci = lax.broadcasted_iota(jnp.int32, (n, n), 1)
    w_ref[:, n:] = jnp.where(ri == ci, 1.0, 0.0)
    full=(SUB,LANE)
    sub=lax.broadcasted_iota(jnp.int32,full,0)
    lane=lax.broadcasted_iota(jnp.int32,full,1)
    zero=jnp.zeros(full,jnp.float32)
    def span(k): return (k//LANE)*LANE, n+((k+SUB+LANE-1)//LANE)*LANE
    def lanebc(x,o): return jnp.broadcast_to(x[:,o:o+1],full)
    def subbc(x,i): return jnp.broadcast_to(x[i:i+1,:],full)
    def load(k):
        lo,hi=span(k)
        P={t: w_ref[k:k+SUB,t*LANE:(t+1)*LANE] for t in range(lo//LANE,hi//LANE)}
        diag={}
        for j in range(SUB):
            c=lanebc(P[lo//LANE],k-lo+j)
            for i in range(j+1): diag[i,j]=subbc(c,i)
        return P,diag
    def loadp(k):
        lo,hi=span(k)
        return {t: w_ref[k:k+SUB,t*LANE:(t+1)*LANE] for t in range(lo//LANE,hi//LANE)}
    def diagof(P,k):
        diag={}
        for j in range(SUB):
            c=lanebc(P[k//LANE],k%LANE+j)
            for i in range(j+1): diag[i,j]=subbc(c,i)
        return diag
    def split3(x):
        h=x.astype(jnp.bfloat16); x=x-h.astype(jnp.float32)
        m=x.astype(jnp.bfloat16); x=x-m.astype(jnp.float32)
        return h,m,x.astype(jnp.bfloat16)
    coming={k: loadp(k) for k in range(0,min(DEPTH*SUB,n),SUB)}
    diag=diagof(coming[0],0)
    for k in range(0,n,SUB):
        lo,hi=span(k)
        tiles=range(lo//LANE,hi//LANE)
        nxt=k+SUB
        P=coming.pop(k)
        if nxt<n: ndiag=diagof(coming[nxt],nxt) if DEPTH>1 else None
        roots=zero
        for i in range(SUB):
            r=lax.rsqrt(diag[i,i])
            roots=jnp.where(sub==i,r,roots)
            if i<SUB-1:
                col=zero
                for j in range(i+1,SUB): col=jnp.where(sub==j,diag[i,j],col)
                col=col*(r*r)
                s={j: diag[i,j]*r for j in range(i+1,SUB)}
                for j in range(i+1,SUB):
                    for l in range(j,SUB): diag[j,l]=diag[j,l]-s[j]*s[l]
                for t in tiles: P[t]=P[t]-col*subbc(P[t],i)
        t0=lo//LANE
        done={t: P[t]*roots for t in tiles}
        done[t0]=jnp.where(lane>=(k-lo)+sub,done[t0],0.0)
        far=k+DEPTH*SUB
        if far<n: coming[far]=loadp(far)
        if nxt<n:
            tn,on=nxt//LANE,nxt%LANE
            E=[lanebc(done[tn],on+j) for j in range(SUB)]
            for i in range(SUB):
                for j in range(i,SUB):
                    ndiag[i,j]=ndiag[i,j]-jnp.broadcast_to(jnp.sum(E[i]*E[j],axis=0,keepdims=True),full)
            for kk in range(SUB):
                row={t: subbc(done[t],kk) for t in done}
                for q in coming:
                    tq,oq=q//LANE,q%LANE
                    c=jnp.sum(jnp.where(lane==oq+sub,row[tq],0.0),axis=1,keepdims=True)
                    c=jnp.broadcast_to(c,full)
                    for t in row:
                        if t in coming[q]: coming[q][t]=coming[q][t]-c*row[t]
        U=jnp.concatenate([done[t] for t in tiles],axis=1)
        if lo: u_ref[k:k+SUB,:lo]=jnp.zeros((SUB,lo),jnp.float32)
        u_ref[k:k+SUB,lo:]=U[:,:n-lo]
        v_ref[k:k+SUB,:hi-n]=U[:,n-lo:]
        if hi<2*n: v_ref[k:k+SUB,hi-n:]=jnp.zeros((SUB,2*n-hi),jnp.float32)
        below=far+SUB
        if below<n:
            lane1=(below//LANE)*LANE
            h,m,l=split3(U[:,lane1-lo:])
            lhs=jnp.concatenate([x[:,:n-lane1].astype(jnp.float32) for x in (h,h,m,h,l,m)],axis=0).astype(jnp.bfloat16)
            rhs=jnp.concatenate([x.astype(jnp.float32) for x in (h,m,h,l,h,m)],axis=0).astype(jnp.bfloat16)
            M=lax.dot_general(lhs,rhs,(((0,),(0,)),((),())),preferred_element_type=jnp.float32)
            w_ref[below:, lane1:hi]=w_ref[below:, lane1:hi]-M[below-lane1:,:]
        if nxt<n: diag=ndiag


def factored(place, own, other, scale):
    n = own.shape[-1] * 2
    return pl.pallas_call(
        functools.partial(factor_kernel, scale),
        in_specs=[SCALARS, WHOLE, WHOLE],
        out_specs=(WHOLE, WHOLE),
        out_shape=(floats(n, n), floats(n, n)),
        scratch_shapes=[pltpu.VMEM((n, 2 * n), jnp.float32)],
        compiler_params=LIMIT,
        name="factor",
    )(place, own, other)


def terms_kernel(*refs):
    count = len(refs) // 3
    for which in range(count):
        high, low = split(refs[which][...])
        refs[count + 2 * which][...] = high
        refs[count + 2 * which + 1][...] = low


def terms_of(slabs, part=0, parts=1):
    depth, n, _ = slabs[0].shape
    depth = depth // parts
    step = 2 if depth % 2 == 0 else 1
    first = part * depth // step
    block = pl.BlockSpec((step, n, n), lambda g: (g, 0, 0))
    outs = pl.pallas_call(
        terms_kernel,
        grid=(depth // step,),
        in_specs=[pl.BlockSpec((step, n, n), lambda g: (first + g, 0, 0))] * len(slabs),
        out_specs=[block] * (2 * len(slabs)),
        out_shape=[jax.ShapeDtypeStruct((depth, n, n), jnp.bfloat16)] * (2 * len(slabs)),
        compiler_params=LIMIT,
        name="terms",
    )(*slabs)
    return [tuple(outs[2 * which : 2 * which + 2]) for which in range(len(slabs))]


def turn_kernel(factor_ref, *refs):
    factor = split(factor_ref[...])
    out_ref = refs[-1]
    for which in range(len(refs) // 2):
        high_ref, low_ref = refs[2 * which : 2 * which + 2]
        for a in range(high_ref.shape[0]):
            turned = product(factor, (high_ref[a], low_ref[a]), ((1,), (0,)))
            out_ref[:, which, a] = turned.reshape(
                out_ref.shape[0], out_ref.shape[3], out_ref.shape[4]
            )


def turned_by(factor, slabs, dests):
    depth, n, _ = slabs[0][0].shape
    cols = factor.shape[0] // dests
    if cols % SUB:
        wide = [high.astype(jnp.float32) + low.astype(jnp.float32) for high, low in slabs]
        rows = factor.reshape(dests, cols, n)
        return jnp.einsum("djb,sabk->dsajk", rows, jnp.stack(wide), precision=FAST)
    step = max(1, 4 // len(slabs))
    step = step if depth % step == 0 else 1
    return pl.pallas_call(
        turn_kernel,
        grid=(depth // step,),
        in_specs=[pl.BlockSpec(factor.shape, lambda g: (0, 0))]
        + [pl.BlockSpec((step, n, n), lambda g: (g, 0, 0))] * (2 * len(slabs)),
        out_specs=pl.BlockSpec((dests, len(slabs), step, cols, n), lambda g: (0, 0, g, 0, 0)),
        out_shape=pltpu.HBM((dests, len(slabs), depth, cols, n), jnp.float32),
        compiler_params=LIMIT,
        name="turn",
    )(factor, *[term for slab in slabs for term in slab])


def move_kernel(place_ref, factor_ref, x_ref, y_ref, *refs):
    moved_refs, (kept_ref, sent_ref, terms_ref) = refs[:-3], refs[-3:]
    step = pl.program_id(0)

    @pl.when(step == 0)
    def _():
        terms_ref[...] = jnp.zeros_like(terms_ref)

    factor = split(factor_ref[...])
    depth, cols, lanes = x_ref.shape
    flat = [ref.reshape(depth * cols, lanes) for ref in (x_ref, y_ref)]
    terms = terms_ref[...]
    for s in range(cols):
        parts = [ref[pl.ds(s, depth, stride=cols), :] for ref in flat]
        moved = product(factor, split(jnp.concatenate(parts, axis=1)), ((1,), (0,)))
        rows = depth // len(moved_refs)
        for which, ref in enumerate(moved_refs):
            ref[s] = moved[which * rows : (which + 1) * rows]
        terms = terms + gram_terms(moved)
    terms_ref[...] = terms

    @pl.when(step == pl.num_programs(0) - 1)
    def _():
        put_parts(gram_of(terms), place_ref[0], kept_ref, sent_ref)


def moved_by(place, factor, gathered, outputs):
    depth, cols, n = gathered.shape
    part = packed_shape(n)
    if cols % SUB:
        moved = jnp.einsum("ia,ajk->jik", factor, gathered, precision=FAST)
        flat = moved.reshape(-1, n)
        gram = jnp.einsum("rc,rd->cd", flat, flat, precision=lax.Precision.HIGHEST)
        parts = packed(gram, 0), packed(gram, 1)
        first = place[0] == 0
        kept, sent = jnp.where(first, *parts), jnp.where(first, *parts[::-1])
        return (*jnp.split(moved, outputs, axis=1), kept, sent)
    rows = depth // outputs
    return pl.pallas_call(
        move_kernel,
        grid=(cols // SUB,),
        in_specs=[
            SCALARS,
            pl.BlockSpec(factor.shape, lambda g: (0, 0)),
            pl.BlockSpec((depth, SUB, n // 2), lambda g: (0, g, 0)),
            pl.BlockSpec((depth, SUB, n // 2), lambda g: (0, g, 1)),
        ],
        out_specs=[pl.BlockSpec((SUB, rows, n), lambda g: (g, 0, 0))] * outputs
        + [pl.BlockSpec(part.shape, lambda g: (0, 0))] * 2,
        out_shape=[pltpu.HBM((cols, rows, n), jnp.float32)] * outputs + [part, part],
        scratch_shapes=[pltpu.VMEM((n, 2 * n), jnp.float32)],
        compiler_params=LIMIT,
        name="move",
    )(place, factor, gathered, gathered)


def base_kernel(inverse_ref, moved_ref, out_ref):
    inverse = split(inverse_ref[...])
    cols, rows, _ = moved_ref.shape
    flat = out_ref.reshape(rows * cols, out_ref.shape[2])
    for s in range(cols):
        flat[pl.ds(s, rows, stride=cols), :] = product(split(moved_ref[s]), inverse, ((1,), (1,)))


def bases_of(inverse, moved):
    cols, rows, n = moved.shape
    if cols % SUB:
        return jnp.einsum("jik,lk->ijl", moved, inverse, precision=FAST)
    return pl.pallas_call(
        base_kernel,
        grid=(cols // SUB, 2),
        in_specs=[
            pl.BlockSpec((n // 2, n), lambda g, h: (h, 0)),
            pl.BlockSpec((SUB, rows, n), lambda g, h: (g, 0, 0)),
        ],
        out_specs=pl.BlockSpec((rows, SUB, n // 2), lambda g, h: (0, g, h)),
        out_shape=floats(rows, cols, n),
        compiler_params=LIMIT,
        name="bases",
    )(inverse, moved)


def joined_kernel(node_ref, inverse_ref, mine_ref, other_ref, out_ref):
    inverse = split(inverse_ref[...])
    cols, rows, _ = mine_ref.shape
    flat = out_ref.reshape(rows * cols, out_ref.shape[2])
    own = pl.program_id(0) == node_ref[0]
    for s in range(cols):
        moved = jnp.where(own, mine_ref[s], other_ref[s])
        flat[pl.ds(s, rows, stride=cols), :] = product(split(moved), inverse, ((1,), (1,)))


def joined_bases(node, inverse, mine, other):
    cols, rows, n = mine.shape
    if cols % SUB:
        left = node[0] == 0
        first, second = jnp.where(left, mine, other), jnp.where(left, other, mine)
        return bases_of(inverse, jnp.concatenate([first, second]))
    return pl.pallas_call(
        joined_kernel,
        grid=(2, 2),
        in_specs=[SCALARS, pl.BlockSpec((n // 2, n), lambda g, h: (h, 0))]
        + [pl.BlockSpec((cols, rows, n), lambda g, h: (0, 0, 0))] * 2,
        out_specs=pl.BlockSpec((rows, cols, n // 2), lambda g, h: (0, g, h)),
        out_shape=floats(rows, 2 * cols, n),
        compiler_params=LIMIT,
        name="joined_bases",
    )(node, inverse, mine, other)


def masks_of():
    masks = [1]
    while 2 * masks[-1] < lax.axis_size("row"):
        masks.append(2 * masks[-1])
    return masks


def first_round(kept, sent):
    return kept + swapped(sent, "row", 1)


def later_rounds(total):
    for mask in masks_of()[1:]:
        total = total + swapped(total, "row", mask)
    return total


def tied(one, other):
    return lax.optimization_barrier((one, other))


def sorted_by(factor, rows_from, cols_from):
    n = factor.shape[0]
    ids = jnp.arange(n, dtype=jnp.int32)
    high = lax.Precision.HIGHEST
    chosen = (ids[:, None] == cols_from[None, :]).astype(jnp.float32)
    factor = jnp.dot(factor, chosen, precision=high)
    chosen = (rows_from[:, None] == ids[None, :]).astype(jnp.float32)
    return jnp.dot(chosen, factor, precision=high)


def body(leaves, level_one, level_two):
    rows = lax.axis_size("row")
    rank = leaves.shape[-1]
    node = lax.axis_index("node") % 2
    is_left = node == 0
    place = jnp.stack([lax.axis_index("row") % 2]).astype(jnp.int32)

    def factors_of(part, scale):
        return factored(place, part, swapped(part, "row", 1), scale)

    own_two = level_two[0]
    sibling_two = swapped(own_two, "node", 1)

    leaf_scale = 1.0 / (leaves.shape[1] * rows)
    masks = masks_of()
    right_part = first_round(*leaf_partial(place, leaves, 1))
    left_part, left_sent = leaf_partial(place, leaves, 0)
    rounds = [lambda part: part + swapped(left_sent, "row", 1)]
    for mask in masks[1:]:
        rounds.append(lambda part, mask=mask: part + swapped(part, "row", mask))
    slab = in_hbm(level_one[0])
    slabs = []
    for index, mask in enumerate(masks[1:], 1):
        late = index - len(masks) + 2
        if late >= 0:
            slab, right_part, left_part, slabs = lax.optimization_barrier(
                (slab, right_part, left_part, slabs)
            )
            left_part = rounds[late](left_part)
            slabs = slabs + terms_of([in_hbm(slab)], late, 2)
        right_part = right_part + swapped(right_part, "row", mask)
    right_part, left_part, slabs = lax.optimization_barrier((right_part, left_part, slabs))
    right_upper, right_inverse = factors_of(right_part, leaf_scale)
    right_upper, left_part = tied(right_upper, left_part)
    for later in rounds[2:-1]:
        left_part = later(left_part)
    turned = turned_by(right_upper, slabs, rows)
    turned, left_part = tied(turned, left_part)
    gathered = lax.all_to_all(turned, "row", 0, 0, tiled=True)
    left_part = rounds[-1](left_part)
    slabs = terms_of([own_two, sibling_two])

    left_upper, left_inverse = factors_of(left_part, leaf_scale)
    leaf_bases = leaf_bases_of(leaves, left_inverse, right_inverse)
    gathered, leaf_bases, slabs = lax.optimization_barrier((gathered, leaf_bases, slabs))

    cols = gathered.shape[3]
    moved_one, kept, sent = moved_by(place, left_upper, gathered.reshape(rank, cols, rank), 1)
    own_part = later_rounds(first_round(kept, sent))
    sibling_part = swapped(own_part, "node", 1)
    scale = 1.0 / (rank * rank)
    right_upper, right_inverse = factors_of(jnp.where(is_left, sibling_part, own_part), scale)

    chosen = right_upper.reshape(rows, 2, -1, rank).transpose(1, 0, 2, 3)
    chosen = lax.dynamic_index_in_dim(chosen, node, 0, keepdims=False).reshape(-1, rank)
    turned = turned_by(chosen, slabs, rows)
    gathered = lax.all_to_all(turned, "row", 0, 0, tiled=True)

    left_upper, left_inverse = factors_of(jnp.where(is_left, own_part, sibling_part), scale)
    one_inverse = jnp.where(is_left, left_inverse, right_inverse)
    level_one_bases = bases_of(one_inverse, moved_one)[None]
    ids = jnp.arange(rank, dtype=jnp.int32)
    depth = own_two.shape[0]
    rows_from = 2 * (ids % (rank // 2)) + (ids // (rank // 2) + node) % 2
    cols_from = ids // (2 * depth) * (2 * depth) + 2 * (ids % depth) + (ids // depth + node) % 2
    sorted_left = sorted_by(left_upper, rows_from, cols_from)
    gathered, level_one_bases, sorted_left = lax.optimization_barrier(
        (gathered, level_one_bases, sorted_left)
    )

    cols = gathered.shape[3]
    mine, theirs, kept, sent = moved_by(place, sorted_left, gathered.reshape(rank, cols, rank), 2)
    part = first_round(kept, sent)
    part = part + swapped(part, "node", 1)
    theirs, part = tied(theirs, part)
    received = swapped(theirs, "node", 1)
    two_upper, two_inverse = factors_of(later_rounds(part), scale)
    place = jnp.stack([node]).astype(jnp.int32)
    level_two_bases = joined_bases(place, two_inverse, mine, received)[None]
    return (leaf_bases, level_one_bases, level_two_bases, two_upper[None])


def solution(mesh):
    placed = (P("node", "row", None), P("node", "row", None, None), P("node", "row", None, None))
    return jax.shard_map(
        body,
        mesh=mesh,
        in_specs=placed,
        out_specs=(
            P("node", "row", None),
            P("node", None, "row", None),
            P("node", None, "row", None),
            P("node", None, None),
        ),
        check_vma=False,
    )
```

```python
import functools
import jax
import jax.numpy as jnp
from jax import lax
from jax.experimental import pallas as pl
from jax.experimental.pallas import tpu as pltpu
from jax.sharding import PartitionSpec as P

FAST = lax.Precision.HIGH
SUB = 8
LANE = 128
DEPTH = 2
WHOLE = pl.BlockSpec(memory_space=pltpu.VMEM)
SCALARS = pl.BlockSpec(memory_space=pltpu.SMEM)
LIMIT = pltpu.CompilerParams(vmem_limit_bytes=24 * 2**20)


def in_hbm(value):
    return pltpu.with_memory_space_constraint(value, pltpu.HBM)


def floats(*shape):
    return jax.ShapeDtypeStruct(shape, jnp.float32)


def swapped(value, axis, mask):
    pairs = [(source, source ^ mask) for source in range(lax.axis_size(axis))]
    return lax.ppermute(value, axis, pairs)


def split(value):
    high = value.astype(jnp.bfloat16)
    return high, (value - high.astype(jnp.float32)).astype(jnp.bfloat16)


def product(left, right, dims):
    def dot(one, other):
        return lax.dot_general(one, other, (dims, ((), ())), preferred_element_type=jnp.float32)

    if dims[0] == (1,):
        rows = left[0].shape[0]
        both = dot(jnp.concatenate(left, axis=0), right[0])
        return both[:rows] + (dot(left[0], right[1]) + both[rows:])
    return dot(left[0], right[0]) + (dot(left[0], right[1]) + dot(left[1], right[0]))


def gram_terms(value):
    high, low = split(value)
    both = jnp.concatenate([high, low], axis=1)
    return lax.dot_general(
        high, both, (((0,), (0,)), ((), ())), preferred_element_type=jnp.float32
    )


def gram_of(terms):
    n = terms.shape[0]
    return terms[:, :n] + (terms[:, n:] + terms[:, n:].T)


def packed(gram, core):
    half, quarter = gram.shape[0] // 2, gram.shape[0] // 4
    if core == 0:
        square, row, corner = gram[:quarter, :half], gram[:quarter, half:], gram[-quarter:, -quarter:]
    else:
        square, row = gram[half : half + quarter, half:], gram[quarter:half, half:]
        corner = gram[quarter:half, quarter:half]
    corner = jnp.concatenate([corner[: quarter // 2], corner[quarter // 2 :]], axis=1)
    return jnp.concatenate([square, row, corner], axis=0)


def packed_shape(n):
    return floats(n // 4 * 2 + n // 8, n // 2)


def put_parts(gram, core, kept_ref, sent_ref):
    first, second = packed(gram, 0), packed(gram, 1)
    kept_ref[...] = jnp.where(core == 0, first, second)
    sent_ref[...] = jnp.where(core == 0, second, first)


def leaf_kernel(place_ref, leaf_ref, kept_ref, sent_ref):
    _, rows, n = leaf_ref.shape
    step = min(rows, 256)
    terms = jnp.zeros((n, 2 * n), jnp.float32)
    for start in range(0, rows, step):
        terms = terms + gram_terms(leaf_ref[0, start : start + step, :])
    put_parts(gram_of(terms), place_ref[0], kept_ref, sent_ref)


def leaf_partial(place, leaves, leaf):
    _, rows, n = leaves.shape
    part = packed_shape(n)
    return pl.pallas_call(
        leaf_kernel,
        grid=(1,),
        in_specs=[SCALARS, pl.BlockSpec((1, rows, n), lambda g: (leaf, 0, 0))],
        out_specs=(pl.BlockSpec(part.shape, lambda g: (0, 0)),) * 2,
        out_shape=(part, part),
        compiler_params=LIMIT,
        name="leaf_partial",
    )(place, in_hbm(leaves))


def leaf_base_kernel(leaf_ref, first_ref, second_ref, out_ref):
    for leaf, ref in enumerate((first_ref, second_ref)):
        inverse = split(ref[...])
        out_ref[leaf] = product(split(leaf_ref[leaf]), inverse, ((1,), (1,)))


def leaf_bases_of(leaves, first, second):
    count, rows, n = leaves.shape
    step = min(rows, 256)
    return pl.pallas_call(
        leaf_base_kernel,
        grid=(rows // step,),
        in_specs=[pl.BlockSpec((count, step, n), lambda g: (0, g, 0))]
        + [pl.BlockSpec((n, n), lambda g: (0, 0))] * 2,
        out_specs=pl.BlockSpec((count, step, n), lambda g: (0, g, 0)),
        out_shape=floats(count, rows, n),
        compiler_params=LIMIT,
        name="leaf_bases",
    )(in_hbm(leaves), first, second)


def factor_kernel(scale, place_ref, own_ref, other_ref, u_ref, v_ref, w_ref):
    n = u_ref.shape[0]
    half, quarter = n // 2, n // 4
    own, other = own_ref[...] * scale, other_ref[...] * scale
    mine = place_ref[0] == 0
    w_ref[:, :n] = jnp.zeros((n, n), jnp.float32)
    for core, part in ((0, jnp.where(mine, own, other)), (1, jnp.where(mine, other, own))):
        square, row, corner = part[:quarter], part[quarter:half], part[half:]
        corner = jnp.concatenate([corner[:, :quarter], corner[:, quarter:]], axis=0)
        start = core * half
        w_ref[start : start + quarter, start : start + half] = square
        w_ref[core * quarter : (core + 1) * quarter, half:n] = row
        start = n - quarter if core == 0 else quarter
        w_ref[start : start + quarter, start : start + quarter] = corner
    ri = lax.broadcasted_iota(jnp.int32, (n, n), 0)
    ci = lax.broadcasted_iota(jnp.int32, (n, n), 1)
    w_ref[:, n:] = jnp.where(ri == ci, 1.0, 0.0)
    full=(SUB,LANE)
    sub=lax.broadcasted_iota(jnp.int32,full,0)
    lane=lax.broadcasted_iota(jnp.int32,full,1)
    zero=jnp.zeros(full,jnp.float32)
    def span(k): return (k//LANE)*LANE, n+((k+SUB+LANE-1)//LANE)*LANE
    def lanebc(x,o): return jnp.broadcast_to(x[:,o:o+1],full)
    def subbc(x,i): return jnp.broadcast_to(x[i:i+1,:],full)
    def load(k):
        lo,hi=span(k)
        P={t: w_ref[k:k+SUB,t*LANE:(t+1)*LANE] for t in range(lo//LANE,hi//LANE)}
        diag={}
        for j in range(SUB):
            c=lanebc(P[lo//LANE],k-lo+j)
            for i in range(j+1): diag[i,j]=subbc(c,i)
        return P,diag
    def loadp(k):
        lo,hi=span(k)
        return {t: w_ref[k:k+SUB,t*LANE:(t+1)*LANE] for t in range(lo//LANE,hi//LANE)}
    def diagof(P,k):
        diag={}
        for j in range(SUB):
            c=lanebc(P[k//LANE],k%LANE+j)
            for i in range(j+1): diag[i,j]=subbc(c,i)
        return diag
    def split3(x):
        h=x.astype(jnp.bfloat16); x=x-h.astype(jnp.float32)
        m=x.astype(jnp.bfloat16); x=x-m.astype(jnp.float32)
        return h,m,x.astype(jnp.bfloat16)
    coming={k: loadp(k) for k in range(0,min(DEPTH*SUB,n),SUB)}
    diag=diagof(coming[0],0)
    for k in range(0,n,SUB):
        lo,hi=span(k)
        tiles=range(lo//LANE,hi//LANE)
        nxt=k+SUB
        P=coming.pop(k)
        if nxt<n: ndiag=diagof(coming[nxt],nxt) if DEPTH>1 else None
        roots=zero
        for i in range(SUB):
            r=lax.rsqrt(diag[i,i])
            roots=jnp.where(sub==i,r,roots)
            if i<SUB-1:
                col=zero
                for j in range(i+1,SUB): col=jnp.where(sub==j,diag[i,j],col)
                col=col*(r*r)
                s={j: diag[i,j]*r for j in range(i+1,SUB)}
                for j in range(i+1,SUB):
                    for l in range(j,SUB): diag[j,l]=diag[j,l]-s[j]*s[l]
                for t in tiles: P[t]=P[t]-col*subbc(P[t],i)
        t0=lo//LANE
        done={t: P[t]*roots for t in tiles}
        done[t0]=jnp.where(lane>=(k-lo)+sub,done[t0],0.0)
        far=k+DEPTH*SUB
        if far<n: coming[far]=loadp(far)
        if nxt<n:
            tn,on=nxt//LANE,nxt%LANE
            E=[lanebc(done[tn],on+j) for j in range(SUB)]
            for i in range(SUB):
                for j in range(i,SUB):
                    ndiag[i,j]=ndiag[i,j]-jnp.broadcast_to(jnp.sum(E[i]*E[j],axis=0,keepdims=True),full)
            for kk in range(SUB):
                row={t: subbc(done[t],kk) for t in done}
                for q in coming:
                    tq,oq=q//LANE,q%LANE
                    c=jnp.sum(jnp.where(lane==oq+sub,row[tq],0.0),axis=1,keepdims=True)
                    c=jnp.broadcast_to(c,full)
                    for t in row:
                        if t in coming[q]: coming[q][t]=coming[q][t]-c*row[t]
        U=jnp.concatenate([done[t] for t in tiles],axis=1)
        if lo: u_ref[k:k+SUB,:lo]=jnp.zeros((SUB,lo),jnp.float32)
        u_ref[k:k+SUB,lo:]=U[:,:n-lo]
        v_ref[k:k+SUB,:hi-n]=U[:,n-lo:]
        if hi<2*n: v_ref[k:k+SUB,hi-n:]=jnp.zeros((SUB,2*n-hi),jnp.float32)
        below=far+SUB
        if below<n:
            lane1=(below//LANE)*LANE
            h,m,l=split3(U[:,lane1-lo:])
            lhs=jnp.concatenate([x[:,:n-lane1].astype(jnp.float32) for x in (h,h,m,h,l,m)],axis=0).astype(jnp.bfloat16)
            rhs=jnp.concatenate([x.astype(jnp.float32) for x in (h,m,h,l,h,m)],axis=0).astype(jnp.bfloat16)
            M=lax.dot_general(lhs,rhs,(((0,),(0,)),((),())),preferred_element_type=jnp.float32)
            w_ref[below:, lane1:hi]=w_ref[below:, lane1:hi]-M[below-lane1:,:]
        if nxt<n: diag=ndiag


def factored(place, own, other, scale):
    n = own.shape[-1] * 2
    return pl.pallas_call(
        functools.partial(factor_kernel, scale),
        in_specs=[SCALARS, WHOLE, WHOLE],
        out_specs=(WHOLE, WHOLE),
        out_shape=(floats(n, n), floats(n, n)),
        scratch_shapes=[pltpu.VMEM((n, 2 * n), jnp.float32)],
        compiler_params=LIMIT,
        name="factor",
    )(place, own, other)


def terms_kernel(*refs):
    count = len(refs) // 3
    for which in range(count):
        high, low = split(refs[which][...])
        refs[count + 2 * which][...] = high
        refs[count + 2 * which + 1][...] = low


def terms_of(slabs, part=0, parts=1):
    depth, n, _ = slabs[0].shape
    depth = depth // parts
    step = 2 if depth % 2 == 0 else 1
    first = part * depth // step
    block = pl.BlockSpec((step, n, n), lambda g: (g, 0, 0))
    outs = pl.pallas_call(
        terms_kernel,
        grid=(depth // step,),
        in_specs=[pl.BlockSpec((step, n, n), lambda g: (first + g, 0, 0))] * len(slabs),
        out_specs=[block] * (2 * len(slabs)),
        out_shape=[jax.ShapeDtypeStruct((depth, n, n), jnp.bfloat16)] * (2 * len(slabs)),
        compiler_params=LIMIT,
        name="terms",
    )(*slabs)
    return [tuple(outs[2 * which : 2 * which + 2]) for which in range(len(slabs))]


def turn_kernel(factor_ref, *refs):
    factor = split(factor_ref[...])
    out_ref = refs[-1]
    for which in range(len(refs) // 2):
        high_ref, low_ref = refs[2 * which : 2 * which + 2]
        for a in range(high_ref.shape[0]):
            turned = product(factor, (high_ref[a], low_ref[a]), ((1,), (0,)))
            out_ref[:, which, a] = turned.reshape(
                out_ref.shape[0], out_ref.shape[3], out_ref.shape[4]
            )


def turned_by(factor, slabs, dests):
    depth, n, _ = slabs[0][0].shape
    cols = factor.shape[0] // dests
    if cols % SUB:
        wide = [high.astype(jnp.float32) + low.astype(jnp.float32) for high, low in slabs]
        rows = factor.reshape(dests, cols, n)
        return jnp.einsum("djb,sabk->dsajk", rows, jnp.stack(wide), precision=FAST)
    step = max(1, 4 // len(slabs))
    step = step if depth % step == 0 else 1
    return pl.pallas_call(
        turn_kernel,
        grid=(depth // step,),
        in_specs=[pl.BlockSpec(factor.shape, lambda g: (0, 0))]
        + [pl.BlockSpec((step, n, n), lambda g: (g, 0, 0))] * (2 * len(slabs)),
        out_specs=pl.BlockSpec((dests, len(slabs), step, cols, n), lambda g: (0, 0, g, 0, 0)),
        out_shape=pltpu.HBM((dests, len(slabs), depth, cols, n), jnp.float32),
        compiler_params=LIMIT,
        name="turn",
    )(factor, *[term for slab in slabs for term in slab])


def move_kernel(place_ref, factor_ref, x_ref, y_ref, *refs):
    moved_refs, (kept_ref, sent_ref, terms_ref) = refs[:-3], refs[-3:]
    step = pl.program_id(0)

    @pl.when(step == 0)
    def _():
        terms_ref[...] = jnp.zeros_like(terms_ref)

    factor = split(factor_ref[...])
    depth, cols, lanes = x_ref.shape
    flat = [ref.reshape(depth * cols, lanes) for ref in (x_ref, y_ref)]
    terms = terms_ref[...]
    for s in range(cols):
        parts = [ref[pl.ds(s, depth, stride=cols), :] for ref in flat]
        moved = product(factor, split(jnp.concatenate(parts, axis=1)), ((1,), (0,)))
        rows = depth // len(moved_refs)
        for which, ref in enumerate(moved_refs):
            ref[s] = moved[which * rows : (which + 1) * rows]
        terms = terms + gram_terms(moved)
    terms_ref[...] = terms

    @pl.when(step == pl.num_programs(0) - 1)
    def _():
        put_parts(gram_of(terms), place_ref[0], kept_ref, sent_ref)


def moved_by(place, factor, gathered, outputs):
    depth, cols, n = gathered.shape
    part = packed_shape(n)
    if cols % SUB:
        moved = jnp.einsum("ia,ajk->jik", factor, gathered, precision=FAST)
        flat = moved.reshape(-1, n)
        gram = jnp.einsum("rc,rd->cd", flat, flat, precision=lax.Precision.HIGHEST)
        parts = packed(gram, 0), packed(gram, 1)
        first = place[0] == 0
        kept, sent = jnp.where(first, *parts), jnp.where(first, *parts[::-1])
        return (*jnp.split(moved, outputs, axis=1), kept, sent)
    rows = depth // outputs
    return pl.pallas_call(
        move_kernel,
        grid=(cols // SUB,),
        in_specs=[
            SCALARS,
            pl.BlockSpec(factor.shape, lambda g: (0, 0)),
            pl.BlockSpec((depth, SUB, n // 2), lambda g: (0, g, 0)),
            pl.BlockSpec((depth, SUB, n // 2), lambda g: (0, g, 1)),
        ],
        out_specs=[pl.BlockSpec((SUB, rows, n), lambda g: (g, 0, 0))] * outputs
        + [pl.BlockSpec(part.shape, lambda g: (0, 0))] * 2,
        out_shape=[floats(cols, rows, n)] * (outputs - 1)
        + [pltpu.HBM((cols, rows, n), jnp.float32), part, part],
        scratch_shapes=[pltpu.VMEM((n, 2 * n), jnp.float32)],
        compiler_params=LIMIT,
        name="move",
    )(place, factor, gathered, gathered)


def base_kernel(inverse_ref, moved_ref, out_ref):
    inverse = split(inverse_ref[...])
    cols, rows, _ = moved_ref.shape
    flat = out_ref.reshape(rows * cols, out_ref.shape[2])
    for s in range(cols):
        flat[pl.ds(s, rows, stride=cols), :] = product(split(moved_ref[s]), inverse, ((1,), (1,)))


def bases_of(inverse, moved):
    cols, rows, n = moved.shape
    if cols % SUB:
        return jnp.einsum("jik,lk->ijl", moved, inverse, precision=FAST)
    return pl.pallas_call(
        base_kernel,
        grid=(cols // SUB, 2),
        in_specs=[
            pl.BlockSpec((n // 2, n), lambda g, h: (h, 0)),
            pl.BlockSpec((SUB, rows, n), lambda g, h: (g, 0, 0)),
        ],
        out_specs=pl.BlockSpec((rows, SUB, n // 2), lambda g, h: (0, g, h)),
        out_shape=floats(rows, cols, n),
        compiler_params=LIMIT,
        name="bases",
    )(inverse, moved)


def joined_kernel(node_ref, inverse_ref, mine_ref, other_ref, out_ref):
    inverse = split(inverse_ref[...])
    cols, rows, _ = mine_ref.shape
    flat = out_ref.reshape(rows * cols, out_ref.shape[2])
    own = pl.program_id(0) == node_ref[0]
    for s in range(cols):
        moved = jnp.where(own, mine_ref[s], other_ref[s])
        flat[pl.ds(s, rows, stride=cols), :] = product(split(moved), inverse, ((1,), (1,)))


def joined_bases(node, inverse, mine, other):
    cols, rows, n = mine.shape
    if cols % SUB:
        left = node[0] == 0
        first, second = jnp.where(left, mine, other), jnp.where(left, other, mine)
        return bases_of(inverse, jnp.concatenate([first, second]))
    return pl.pallas_call(
        joined_kernel,
        grid=(2, 2),
        in_specs=[SCALARS, pl.BlockSpec((n // 2, n), lambda g, h: (h, 0))]
        + [pl.BlockSpec((cols, rows, n), lambda g, h: (0, 0, 0))] * 2,
        out_specs=pl.BlockSpec((rows, cols, n // 2), lambda g, h: (0, g, h)),
        out_shape=floats(rows, 2 * cols, n),
        compiler_params=LIMIT,
        name="joined_bases",
    )(node, inverse, mine, other)


def masks_of():
    masks = [1]
    while 2 * masks[-1] < lax.axis_size("row"):
        masks.append(2 * masks[-1])
    return masks


def first_round(kept, sent):
    return kept + swapped(sent, "row", 1)


def later_rounds(total):
    for mask in masks_of()[1:]:
        total = total + swapped(total, "row", mask)
    return total


def tied(one, other):
    return lax.optimization_barrier((one, other))


def sorted_by(factor, rows_from, cols_from):
    n = factor.shape[0]
    ids = jnp.arange(n, dtype=jnp.int32)
    high = lax.Precision.HIGHEST
    chosen = (ids[:, None] == cols_from[None, :]).astype(jnp.float32)
    factor = jnp.dot(factor, chosen, precision=high)
    chosen = (rows_from[:, None] == ids[None, :]).astype(jnp.float32)
    return jnp.dot(chosen, factor, precision=high)


def body(leaves, level_one, level_two):
    rows = lax.axis_size("row")
    rank = leaves.shape[-1]
    node = lax.axis_index("node") % 2
    is_left = node == 0
    place = jnp.stack([lax.axis_index("row") % 2]).astype(jnp.int32)

    def factors_of(part, scale):
        return factored(place, part, swapped(part, "row", 1), scale)

    own_two = level_two[0]
    sibling_two = swapped(own_two, "node", 1)

    leaf_scale = 1.0 / (leaves.shape[1] * rows)
    masks = masks_of()
    right_part = first_round(*leaf_partial(place, leaves, 1))
    left_part, left_sent = leaf_partial(place, leaves, 0)
    rounds = [lambda part: part + swapped(left_sent, "row", 1)]
    for mask in masks[2:] + masks[1:2]:
        rounds.append(lambda part, mask=mask: part + swapped(part, "row", mask))
    slab = in_hbm(level_one[0])
    slabs = []
    for index, mask in enumerate(masks[1:], 1):
        late = index - len(masks) + 2
        if late >= 0:
            slab, right_part, left_part, slabs = lax.optimization_barrier(
                (slab, right_part, left_part, slabs)
            )
            left_part = rounds[late](left_part)
            slabs = slabs + terms_of([in_hbm(slab)], late, 2)
        right_part = right_part + swapped(right_part, "row", mask)
    right_part, left_part, slabs = lax.optimization_barrier((right_part, left_part, slabs))
    right_upper, right_inverse = factors_of(right_part, leaf_scale)
    right_upper, left_part = tied(right_upper, left_part)
    for later in rounds[2:-1]:
        left_part = later(left_part)
    turned = turned_by(right_upper, slabs, rows)
    turned, left_part = tied(turned, left_part)
    gathered = lax.all_to_all(turned, "row", 0, 0, tiled=True)
    left_part = rounds[-1](left_part)
    slabs = terms_of([own_two, sibling_two])

    left_upper, left_inverse = factors_of(left_part, leaf_scale)
    leaf_bases = leaf_bases_of(leaves, left_inverse, right_inverse)
    gathered, leaf_bases, slabs = lax.optimization_barrier((gathered, leaf_bases, slabs))

    cols = gathered.shape[3]
    moved_one, kept, sent = moved_by(place, left_upper, gathered.reshape(rank, cols, rank), 1)
    own_part = later_rounds(first_round(kept, sent))
    sibling_part = swapped(own_part, "node", 1)
    scale = 1.0 / (rank * rank)
    right_upper, right_inverse = factors_of(jnp.where(is_left, sibling_part, own_part), scale)

    chosen = right_upper.reshape(rows, 2, -1, rank).transpose(1, 0, 2, 3)
    chosen = lax.dynamic_index_in_dim(chosen, node, 0, keepdims=False).reshape(-1, rank)
    turned = turned_by(chosen, slabs, rows)
    gathered = lax.all_to_all(turned, "row", 0, 0, tiled=True)

    left_upper, left_inverse = factors_of(jnp.where(is_left, own_part, sibling_part), scale)
    one_inverse = jnp.where(is_left, left_inverse, right_inverse)
    level_one_bases = bases_of(one_inverse, moved_one)[None]
    ids = jnp.arange(rank, dtype=jnp.int32)
    depth = own_two.shape[0]
    rows_from = 2 * (ids % (rank // 2)) + (ids // (rank // 2) + node) % 2
    cols_from = ids // (2 * depth) * (2 * depth) + 2 * (ids % depth) + (ids // depth + node) % 2
    sorted_left = sorted_by(left_upper, rows_from, cols_from)
    gathered, level_one_bases, sorted_left = lax.optimization_barrier(
        (gathered, level_one_bases, sorted_left)
    )

    cols = gathered.shape[3]
    mine, theirs, kept, sent = moved_by(place, sorted_left, gathered.reshape(rank, cols, rank), 2)
    part = first_round(kept, sent)
    part = part + swapped(part, "node", 1)
    theirs, part = tied(theirs, part)
    received = swapped(theirs, "node", 1)
    two_upper, two_inverse = factors_of(later_rounds(part), scale)
    place = jnp.stack([node]).astype(jnp.int32)
    level_two_bases = joined_bases(place, two_inverse, mine, received)[None]
    return (leaf_bases, level_one_bases, level_two_bases, two_upper[None])


def solution(mesh):
    placed = (P("node", "row", None), P("node", "row", None, None), P("node", "row", None, None))
    return jax.shard_map(
        body,
        mesh=mesh,
        in_specs=placed,
        out_specs=(
            P("node", "row", None),
            P("node", None, "row", None),
            P("node", None, "row", None),
            P("node", None, None),
        ),
        check_vma=False,
    )
```

```python
import functools
import jax
import jax.numpy as jnp
from jax import lax
from jax.experimental import pallas as pl
from jax.experimental.pallas import tpu as pltpu
from jax.sharding import PartitionSpec as P

FAST = lax.Precision.HIGH
SUB = 8
LANE = 128
DEPTH = 2
WHOLE = pl.BlockSpec(memory_space=pltpu.VMEM)
SCALARS = pl.BlockSpec(memory_space=pltpu.SMEM)
LIMIT = pltpu.CompilerParams(vmem_limit_bytes=24 * 2**20)


def in_hbm(value):
    return pltpu.with_memory_space_constraint(value, pltpu.HBM)


def floats(*shape):
    return jax.ShapeDtypeStruct(shape, jnp.float32)


def swapped(value, axis, mask):
    pairs = [(source, source ^ mask) for source in range(lax.axis_size(axis))]
    return lax.ppermute(value, axis, pairs)


def split(value):
    high = value.astype(jnp.bfloat16)
    return high, (value - high.astype(jnp.float32)).astype(jnp.bfloat16)


def product(left, right, dims):
    def dot(one, other):
        return lax.dot_general(one, other, (dims, ((), ())), preferred_element_type=jnp.float32)

    if dims[0] == (1,):
        rows = left[0].shape[0]
        both = dot(jnp.concatenate(left, axis=0), right[0])
        return both[:rows] + (dot(left[0], right[1]) + both[rows:])
    return dot(left[0], right[0]) + (dot(left[0], right[1]) + dot(left[1], right[0]))


def gram_terms(value):
    high, low = split(value)
    both = jnp.concatenate([high, low], axis=1)
    return lax.dot_general(
        high, both, (((0,), (0,)), ((), ())), preferred_element_type=jnp.float32
    )


def gram_of(terms):
    n = terms.shape[0]
    return terms[:, :n] + (terms[:, n:] + terms[:, n:].T)


def packed(gram, core):
    half, quarter = gram.shape[0] // 2, gram.shape[0] // 4
    if core == 0:
        square, row, corner = gram[:quarter, :half], gram[:quarter, half:], gram[-quarter:, -quarter:]
    else:
        square, row = gram[half : half + quarter, half:], gram[quarter:half, half:]
        corner = gram[quarter:half, quarter:half]
    corner = jnp.concatenate([corner[: quarter // 2], corner[quarter // 2 :]], axis=1)
    return jnp.concatenate([square, row, corner], axis=0)


def packed_shape(n):
    return floats(n // 4 * 2 + n // 8, n // 2)


def put_parts(gram, core, kept_ref, sent_ref):
    first, second = packed(gram, 0), packed(gram, 1)
    kept_ref[...] = jnp.where(core == 0, first, second)
    sent_ref[...] = jnp.where(core == 0, second, first)


def leaf_kernel(place_ref, leaf_ref, kept_ref, sent_ref):
    _, rows, n = leaf_ref.shape
    step = min(rows, 256)
    terms = jnp.zeros((n, 2 * n), jnp.float32)
    for start in range(0, rows, step):
        terms = terms + gram_terms(leaf_ref[0, start : start + step, :])
    put_parts(gram_of(terms), place_ref[0], kept_ref, sent_ref)


def leaf_partial(place, leaves, leaf):
    _, rows, n = leaves.shape
    part = packed_shape(n)
    return pl.pallas_call(
        leaf_kernel,
        grid=(1,),
        in_specs=[SCALARS, pl.BlockSpec((1, rows, n), lambda g: (leaf, 0, 0))],
        out_specs=(pl.BlockSpec(part.shape, lambda g: (0, 0)),) * 2,
        out_shape=(part, part),
        compiler_params=LIMIT,
        name="leaf_partial",
    )(place, in_hbm(leaves))


def leaf_base_kernel(leaf_ref, first_ref, second_ref, out_ref):
    for leaf, ref in enumerate((first_ref, second_ref)):
        inverse = split(ref[...])
        out_ref[leaf] = product(split(leaf_ref[leaf]), inverse, ((1,), (1,)))


def leaf_bases_of(leaves, first, second):
    count, rows, n = leaves.shape
    step = min(rows, 256)
    return pl.pallas_call(
        leaf_base_kernel,
        grid=(rows // step,),
        in_specs=[pl.BlockSpec((count, step, n), lambda g: (0, g, 0))]
        + [pl.BlockSpec((n, n), lambda g: (0, 0))] * 2,
        out_specs=pl.BlockSpec((count, step, n), lambda g: (0, g, 0)),
        out_shape=floats(count, rows, n),
        compiler_params=LIMIT,
        name="leaf_bases",
    )(in_hbm(leaves), first, second)


def factor_kernel(scale, place_ref, own_ref, other_ref, u_ref, v_ref, w_ref):
    n = u_ref.shape[0]
    half, quarter = n // 2, n // 4
    own, other = own_ref[...] * scale, other_ref[...] * scale
    mine = place_ref[0] == 0
    w_ref[:, :n] = jnp.zeros((n, n), jnp.float32)
    for core, part in ((0, jnp.where(mine, own, other)), (1, jnp.where(mine, other, own))):
        square, row, corner = part[:quarter], part[quarter:half], part[half:]
        corner = jnp.concatenate([corner[:, :quarter], corner[:, quarter:]], axis=0)
        start = core * half
        w_ref[start : start + quarter, start : start + half] = square
        w_ref[core * quarter : (core + 1) * quarter, half:n] = row
        start = n - quarter if core == 0 else quarter
        w_ref[start : start + quarter, start : start + quarter] = corner
    ri = lax.broadcasted_iota(jnp.int32, (n, n), 0)
    ci = lax.broadcasted_iota(jnp.int32, (n, n), 1)
    w_ref[:, n:] = jnp.where(ri == ci, 1.0, 0.0)
    full=(SUB,LANE)
    sub=lax.broadcasted_iota(jnp.int32,full,0)
    lane=lax.broadcasted_iota(jnp.int32,full,1)
    zero=jnp.zeros(full,jnp.float32)
    def span(k): return (k//LANE)*LANE, n+((k+SUB+LANE-1)//LANE)*LANE
    def lanebc(x,o): return jnp.broadcast_to(x[:,o:o+1],full)
    def subbc(x,i): return jnp.broadcast_to(x[i:i+1,:],full)
    def load(k):
        lo,hi=span(k)
        P={t: w_ref[k:k+SUB,t*LANE:(t+1)*LANE] for t in range(lo//LANE,hi//LANE)}
        diag={}
        for j in range(SUB):
            c=lanebc(P[lo//LANE],k-lo+j)
            for i in range(j+1): diag[i,j]=subbc(c,i)
        return P,diag
    def loadp(k):
        lo,hi=span(k)
        return {t: w_ref[k:k+SUB,t*LANE:(t+1)*LANE] for t in range(lo//LANE,hi//LANE)}
    def diagof(P,k):
        diag={}
        for j in range(SUB):
            c=lanebc(P[k//LANE],k%LANE+j)
            for i in range(j+1): diag[i,j]=subbc(c,i)
        return diag
    def split3(x):
        h=x.astype(jnp.bfloat16); x=x-h.astype(jnp.float32)
        m=x.astype(jnp.bfloat16); x=x-m.astype(jnp.float32)
        return h,m,x.astype(jnp.bfloat16)
    coming={k: loadp(k) for k in range(0,min(DEPTH*SUB,n),SUB)}
    diag=diagof(coming[0],0)
    for k in range(0,n,SUB):
        lo,hi=span(k)
        tiles=range(lo//LANE,hi//LANE)
        nxt=k+SUB
        P=coming.pop(k)
        if nxt<n: ndiag=diagof(coming[nxt],nxt) if DEPTH>1 else None
        roots=zero
        for i in range(SUB):
            r=lax.rsqrt(diag[i,i])
            roots=jnp.where(sub==i,r,roots)
            if i<SUB-1:
                col=zero
                for j in range(i+1,SUB): col=jnp.where(sub==j,diag[i,j],col)
                col=col*(r*r)
                s={j: diag[i,j]*r for j in range(i+1,SUB)}
                for j in range(i+1,SUB):
                    for l in range(j,SUB): diag[j,l]=diag[j,l]-s[j]*s[l]
                for t in tiles: P[t]=P[t]-col*subbc(P[t],i)
        t0=lo//LANE
        done={t: P[t]*roots for t in tiles}
        done[t0]=jnp.where(lane>=(k-lo)+sub,done[t0],0.0)
        far=k+DEPTH*SUB
        if far<n: coming[far]=loadp(far)
        if nxt<n:
            tn,on=nxt//LANE,nxt%LANE
            E=[lanebc(done[tn],on+j) for j in range(SUB)]
            for i in range(SUB):
                for j in range(i,SUB):
                    ndiag[i,j]=ndiag[i,j]-jnp.broadcast_to(jnp.sum(E[i]*E[j],axis=0,keepdims=True),full)
            for kk in range(SUB):
                row={t: subbc(done[t],kk) for t in done}
                for q in coming:
                    tq,oq=q//LANE,q%LANE
                    c=jnp.sum(jnp.where(lane==oq+sub,row[tq],0.0),axis=1,keepdims=True)
                    c=jnp.broadcast_to(c,full)
                    for t in row:
                        if t in coming[q]: coming[q][t]=coming[q][t]-c*row[t]
        U=jnp.concatenate([done[t] for t in tiles],axis=1)
        if lo: u_ref[k:k+SUB,:lo]=jnp.zeros((SUB,lo),jnp.float32)
        u_ref[k:k+SUB,lo:]=U[:,:n-lo]
        v_ref[k:k+SUB,:hi-n]=U[:,n-lo:]
        if hi<2*n: v_ref[k:k+SUB,hi-n:]=jnp.zeros((SUB,2*n-hi),jnp.float32)
        below=far+SUB
        if below<n:
            lane1=(below//LANE)*LANE
            h,m,l=split3(U[:,lane1-lo:])
            lhs=jnp.concatenate([x[:,:n-lane1].astype(jnp.float32) for x in (h,h,m,h,l,m)],axis=0).astype(jnp.bfloat16)
            rhs=jnp.concatenate([x.astype(jnp.float32) for x in (h,m,h,l,h,m)],axis=0).astype(jnp.bfloat16)
            M=lax.dot_general(lhs,rhs,(((0,),(0,)),((),())),preferred_element_type=jnp.float32)
            w_ref[below:, lane1:hi]=w_ref[below:, lane1:hi]-M[below-lane1:,:]
        if nxt<n: diag=ndiag


def factored(place, own, other, scale):
    n = own.shape[-1] * 2
    return pl.pallas_call(
        functools.partial(factor_kernel, scale),
        in_specs=[SCALARS, WHOLE, WHOLE],
        out_specs=(WHOLE, WHOLE),
        out_shape=(floats(n, n), floats(n, n)),
        scratch_shapes=[pltpu.VMEM((n, 2 * n), jnp.float32)],
        compiler_params=LIMIT,
        name="factor",
    )(place, own, other)


def terms_kernel(*refs):
    count = len(refs) // 3
    for which in range(count):
        high, low = split(refs[which][...])
        refs[count + 2 * which][...] = high
        refs[count + 2 * which + 1][...] = low


def terms_of(slabs, part=0, parts=1, far=False):
    depth, n, _ = slabs[0].shape
    depth = depth // parts
    step = 2 if depth % 2 == 0 else 1
    first = part * depth // step
    block = pl.BlockSpec((step, n, n), lambda g: (g, 0, 0))
    outs = pl.pallas_call(
        terms_kernel,
        grid=(depth // step,),
        in_specs=[pl.BlockSpec((step, n, n), lambda g: (first + g, 0, 0))] * len(slabs),
        out_specs=[block] * (2 * len(slabs)),
        out_shape=[(pltpu.HBM if far else jax.ShapeDtypeStruct)((depth, n, n), jnp.bfloat16)]
        * (2 * len(slabs)),
        compiler_params=LIMIT,
        name="terms",
    )(*slabs)
    return [tuple(outs[2 * which : 2 * which + 2]) for which in range(len(slabs))]


def turn_kernel(factor_ref, *refs):
    factor = split(factor_ref[...])
    out_ref = refs[-1]
    for which in range(len(refs) // 2):
        high_ref, low_ref = refs[2 * which : 2 * which + 2]
        for a in range(high_ref.shape[0]):
            turned = product(factor, (high_ref[a], low_ref[a]), ((1,), (0,)))
            out_ref[:, which, a] = turned.reshape(
                out_ref.shape[0], out_ref.shape[3], out_ref.shape[4]
            )


def turned_by(factor, slabs, dests):
    depth, n, _ = slabs[0][0].shape
    cols = factor.shape[0] // dests
    if cols % SUB:
        wide = [high.astype(jnp.float32) + low.astype(jnp.float32) for high, low in slabs]
        rows = factor.reshape(dests, cols, n)
        return jnp.einsum("djb,sabk->dsajk", rows, jnp.stack(wide), precision=FAST)
    step = max(1, 4 // len(slabs))
    step = step if depth % step == 0 else 1
    return pl.pallas_call(
        turn_kernel,
        grid=(depth // step,),
        in_specs=[pl.BlockSpec(factor.shape, lambda g: (0, 0))]
        + [pl.BlockSpec((step, n, n), lambda g: (g, 0, 0))] * (2 * len(slabs)),
        out_specs=pl.BlockSpec((dests, len(slabs), step, cols, n), lambda g: (0, 0, g, 0, 0)),
        out_shape=pltpu.HBM((dests, len(slabs), depth, cols, n), jnp.float32),
        compiler_params=LIMIT,
        name="turn",
    )(factor, *[term for slab in slabs for term in slab])


def move_kernel(place_ref, factor_ref, x_ref, y_ref, *refs):
    moved_refs, (kept_ref, sent_ref, terms_ref) = refs[:-3], refs[-3:]
    step = pl.program_id(0)

    @pl.when(step == 0)
    def _():
        terms_ref[...] = jnp.zeros_like(terms_ref)

    factor = split(factor_ref[...])
    depth, cols, lanes = x_ref.shape
    flat = [ref.reshape(depth * cols, lanes) for ref in (x_ref, y_ref)]
    terms = terms_ref[...]
    for s in range(cols):
        parts = [ref[pl.ds(s, depth, stride=cols), :] for ref in flat]
        moved = product(factor, split(jnp.concatenate(parts, axis=1)), ((1,), (0,)))
        rows = depth // len(moved_refs)
        for which, ref in enumerate(moved_refs):
            ref[s] = moved[which * rows : (which + 1) * rows]
        terms = terms + gram_terms(moved)
    terms_ref[...] = terms

    @pl.when(step == pl.num_programs(0) - 1)
    def _():
        put_parts(gram_of(terms), place_ref[0], kept_ref, sent_ref)


def moved_by(place, factor, gathered, outputs):
    depth, cols, n = gathered.shape
    part = packed_shape(n)
    if cols % SUB:
        moved = jnp.einsum("ia,ajk->jik", factor, gathered, precision=FAST)
        flat = moved.reshape(-1, n)
        gram = jnp.einsum("rc,rd->cd", flat, flat, precision=lax.Precision.HIGHEST)
        parts = packed(gram, 0), packed(gram, 1)
        first = place[0] == 0
        kept, sent = jnp.where(first, *parts), jnp.where(first, *parts[::-1])
        return (*jnp.split(moved, outputs, axis=1), kept, sent)
    rows = depth // outputs
    return pl.pallas_call(
        move_kernel,
        grid=(cols // SUB,),
        in_specs=[
            SCALARS,
            pl.BlockSpec(factor.shape, lambda g: (0, 0)),
            pl.BlockSpec((depth, SUB, n // 2), lambda g: (0, g, 0)),
            pl.BlockSpec((depth, SUB, n // 2), lambda g: (0, g, 1)),
        ],
        out_specs=[pl.BlockSpec((SUB, rows, n), lambda g: (g, 0, 0))] * outputs
        + [pl.BlockSpec(part.shape, lambda g: (0, 0))] * 2,
        out_shape=[floats(cols, rows, n)] * (outputs - 1)
        + [pltpu.HBM((cols, rows, n), jnp.float32), part, part],
        scratch_shapes=[pltpu.VMEM((n, 2 * n), jnp.float32)],
        compiler_params=LIMIT,
        name="move",
    )(place, factor, gathered, gathered)


def base_kernel(inverse_ref, moved_ref, out_ref):
    inverse = split(inverse_ref[...])
    cols, rows, _ = moved_ref.shape
    flat = out_ref.reshape(rows * cols, out_ref.shape[2])
    for s in range(cols):
        flat[pl.ds(s, rows, stride=cols), :] = product(split(moved_ref[s]), inverse, ((1,), (1,)))


def bases_of(inverse, moved):
    cols, rows, n = moved.shape
    if cols % SUB:
        return jnp.einsum("jik,lk->ijl", moved, inverse, precision=FAST)
    return pl.pallas_call(
        base_kernel,
        grid=(cols // SUB, 2),
        in_specs=[
            pl.BlockSpec((n // 2, n), lambda g, h: (h, 0)),
            pl.BlockSpec((SUB, rows, n), lambda g, h: (g, 0, 0)),
        ],
        out_specs=pl.BlockSpec((rows, SUB, n // 2), lambda g, h: (0, g, h)),
        out_shape=floats(rows, cols, n),
        compiler_params=LIMIT,
        name="bases",
    )(inverse, moved)


def joined_kernel(node_ref, inverse_ref, mine_ref, other_ref, out_ref):
    inverse = split(inverse_ref[...])
    cols, rows, _ = mine_ref.shape
    flat = out_ref.reshape(rows * cols, out_ref.shape[2])
    own = pl.program_id(0) == node_ref[0]
    for s in range(cols):
        moved = jnp.where(own, mine_ref[s], other_ref[s])
        flat[pl.ds(s, rows, stride=cols), :] = product(split(moved), inverse, ((1,), (1,)))


def joined_bases(node, inverse, mine, other):
    cols, rows, n = mine.shape
    if cols % SUB:
        left = node[0] == 0
        first, second = jnp.where(left, mine, other), jnp.where(left, other, mine)
        return bases_of(inverse, jnp.concatenate([first, second]))
    return pl.pallas_call(
        joined_kernel,
        grid=(2, 2),
        in_specs=[SCALARS, pl.BlockSpec((n // 2, n), lambda g, h: (h, 0))]
        + [pl.BlockSpec((cols, rows, n), lambda g, h: (0, 0, 0))] * 2,
        out_specs=pl.BlockSpec((rows, cols, n // 2), lambda g, h: (0, g, h)),
        out_shape=floats(rows, 2 * cols, n),
        compiler_params=LIMIT,
        name="joined_bases",
    )(node, inverse, mine, other)


def masks_of():
    masks = [1]
    while 2 * masks[-1] < lax.axis_size("row"):
        masks.append(2 * masks[-1])
    return masks


def first_round(kept, sent):
    return kept + swapped(sent, "row", 1)


def later_rounds(total):
    for mask in masks_of()[1:]:
        total = total + swapped(total, "row", mask)
    return total


def tied(one, other):
    return lax.optimization_barrier((one, other))


def sorted_by(factor, rows_from, cols_from):
    n = factor.shape[0]
    ids = jnp.arange(n, dtype=jnp.int32)
    high = lax.Precision.HIGHEST
    chosen = (ids[:, None] == cols_from[None, :]).astype(jnp.float32)
    factor = jnp.dot(factor, chosen, precision=high)
    chosen = (rows_from[:, None] == ids[None, :]).astype(jnp.float32)
    return jnp.dot(chosen, factor, precision=high)


def body(leaves, level_one, level_two):
    rows = lax.axis_size("row")
    rank = leaves.shape[-1]
    node = lax.axis_index("node") % 2
    is_left = node == 0
    place = jnp.stack([lax.axis_index("row") % 2]).astype(jnp.int32)

    def factors_of(part, scale):
        return factored(place, part, swapped(part, "row", 1), scale)

    own_two = level_two[0]
    sibling_two = swapped(own_two, "node", 1)

    leaf_scale = 1.0 / (leaves.shape[1] * rows)
    masks = masks_of()
    right_part = first_round(*leaf_partial(place, leaves, 1))
    left_part, left_sent = leaf_partial(place, leaves, 0)
    rounds = [lambda part: part + swapped(left_sent, "row", 1)]
    for mask in masks[2:] + masks[1:2]:
        rounds.append(lambda part, mask=mask: part + swapped(part, "row", mask))
    slab = in_hbm(level_one[0])
    slabs = []
    for index, mask in enumerate(masks[1:], 1):
        late = index - len(masks) + 2
        if late >= 0:
            slab, right_part, left_part, slabs = lax.optimization_barrier(
                (slab, right_part, left_part, slabs)
            )
            left_part = rounds[late](left_part)
            slabs = slabs + terms_of([in_hbm(slab)], late, 2)
        right_part = right_part + swapped(right_part, "row", mask)
    right_part, left_part, slabs = lax.optimization_barrier((right_part, left_part, slabs))
    right_upper, right_inverse = factors_of(right_part, leaf_scale)
    right_upper, left_part = tied(right_upper, left_part)
    for later in rounds[2:-1]:
        left_part = later(left_part)
    turned = turned_by(right_upper, slabs, rows)
    turned, left_part = tied(turned, left_part)
    gathered = lax.all_to_all(turned, "row", 0, 0, tiled=True)
    left_part = rounds[-1](left_part)
    far = rank // (2 * rows) % SUB == 0
    slabs = terms_of([own_two, sibling_two], far=far)

    left_upper, left_inverse = factors_of(left_part, leaf_scale)
    leaf_bases = leaf_bases_of(leaves, left_inverse, right_inverse)
    gathered, leaf_bases, slabs = lax.optimization_barrier((gathered, leaf_bases, slabs))

    cols = gathered.shape[3]
    moved_one, kept, sent = moved_by(place, left_upper, gathered.reshape(rank, cols, rank), 1)
    own_part = later_rounds(first_round(kept, sent))
    sibling_part = swapped(own_part, "node", 1)
    scale = 1.0 / (rank * rank)
    right_upper, right_inverse = factors_of(jnp.where(is_left, sibling_part, own_part), scale)

    chosen = right_upper.reshape(rows, 2, -1, rank).transpose(1, 0, 2, 3)
    chosen = lax.dynamic_index_in_dim(chosen, node, 0, keepdims=False).reshape(-1, rank)
    if far:
        slabs = [tuple(map(in_hbm, slab)) for slab in slabs]
    turned = turned_by(chosen, slabs, rows)
    gathered = lax.all_to_all(turned, "row", 0, 0, tiled=True)

    left_upper, left_inverse = factors_of(jnp.where(is_left, own_part, sibling_part), scale)
    one_inverse = jnp.where(is_left, left_inverse, right_inverse)
    level_one_bases = bases_of(one_inverse, moved_one)[None]
    ids = jnp.arange(rank, dtype=jnp.int32)
    depth = own_two.shape[0]
    rows_from = 2 * (ids % (rank // 2)) + (ids // (rank // 2) + node) % 2
    cols_from = ids // (2 * depth) * (2 * depth) + 2 * (ids % depth) + (ids // depth + node) % 2
    sorted_left = sorted_by(left_upper, rows_from, cols_from)
    gathered, level_one_bases, sorted_left = lax.optimization_barrier(
        (gathered, level_one_bases, sorted_left)
    )

    cols = gathered.shape[3]
    mine, theirs, kept, sent = moved_by(place, sorted_left, gathered.reshape(rank, cols, rank), 2)
    part = first_round(kept, sent)
    part = part + swapped(part, "node", 1)
    theirs, part = tied(theirs, part)
    received = swapped(theirs, "node", 1)
    two_upper, two_inverse = factors_of(later_rounds(part), scale)
    place = jnp.stack([node]).astype(jnp.int32)
    level_two_bases = joined_bases(place, two_inverse, mine, received)[None]
    return (leaf_bases, level_one_bases, level_two_bases, two_upper[None])


def solution(mesh):
    placed = (P("node", "row", None), P("node", "row", None, None), P("node", "row", None, None))
    return jax.shard_map(
        body,
        mesh=mesh,
        in_specs=placed,
        out_specs=(
            P("node", "row", None),
            P("node", None, "row", None),
            P("node", None, "row", None),
            P("node", None, None),
        ),
        check_vma=False,
    )
```

```python
import functools
import jax
import jax.numpy as jnp
from jax import lax
from jax.experimental import pallas as pl
from jax.experimental.pallas import tpu as pltpu
from jax.sharding import PartitionSpec as P

FAST = lax.Precision.HIGH
SUB = 8
LANE = 128
DEPTH = 2
WHOLE = pl.BlockSpec(memory_space=pltpu.VMEM)
SCALARS = pl.BlockSpec(memory_space=pltpu.SMEM)
LIMIT = pltpu.CompilerParams(vmem_limit_bytes=24 * 2**20)


def in_hbm(value):
    return pltpu.with_memory_space_constraint(value, pltpu.HBM)


def floats(*shape):
    return jax.ShapeDtypeStruct(shape, jnp.float32)


def swapped(value, axis, mask):
    pairs = [(source, source ^ mask) for source in range(lax.axis_size(axis))]
    return lax.ppermute(value, axis, pairs)


def split(value):
    high = value.astype(jnp.bfloat16)
    return high, (value - high.astype(jnp.float32)).astype(jnp.bfloat16)


def product(left, right, dims):
    def dot(one, other):
        return lax.dot_general(one, other, (dims, ((), ())), preferred_element_type=jnp.float32)

    if dims[0] == (1,):
        rows = left[0].shape[0]
        both = dot(jnp.concatenate(left, axis=0), right[0])
        return both[:rows] + (dot(left[0], right[1]) + both[rows:])
    return dot(left[0], right[0]) + (dot(left[0], right[1]) + dot(left[1], right[0]))


def gram_terms(value):
    high, low = split(value)
    both = jnp.concatenate([high, low], axis=1)
    return lax.dot_general(
        high, both, (((0,), (0,)), ((), ())), preferred_element_type=jnp.float32
    )


def gram_of(terms):
    n = terms.shape[0]
    return terms[:, :n] + (terms[:, n:] + terms[:, n:].T)


def packed(gram, core):
    half, quarter = gram.shape[0] // 2, gram.shape[0] // 4
    if core == 0:
        square, row, corner = gram[:quarter, :half], gram[:quarter, half:], gram[-quarter:, -quarter:]
    else:
        square, row = gram[half : half + quarter, half:], gram[quarter:half, half:]
        corner = gram[quarter:half, quarter:half]
    corner = jnp.concatenate([corner[: quarter // 2], corner[quarter // 2 :]], axis=1)
    return jnp.concatenate([square, row, corner], axis=0)


def packed_shape(n):
    return floats(n // 4 * 2 + n // 8, n // 2)


def put_parts(gram, core, kept_ref, sent_ref):
    first, second = packed(gram, 0), packed(gram, 1)
    kept_ref[...] = jnp.where(core == 0, first, second)
    sent_ref[...] = jnp.where(core == 0, second, first)


def leaf_kernel(place_ref, leaf_ref, kept_ref, sent_ref):
    _, rows, n = leaf_ref.shape
    step = min(rows, 256)
    terms = jnp.zeros((n, 2 * n), jnp.float32)
    for start in range(0, rows, step):
        terms = terms + gram_terms(leaf_ref[0, start : start + step, :])
    put_parts(gram_of(terms), place_ref[0], kept_ref, sent_ref)


def leaf_partial(place, leaves, leaf):
    _, rows, n = leaves.shape
    part = packed_shape(n)
    return pl.pallas_call(
        leaf_kernel,
        grid=(1,),
        in_specs=[SCALARS, pl.BlockSpec((1, rows, n), lambda g: (leaf, 0, 0))],
        out_specs=(pl.BlockSpec(part.shape, lambda g: (0, 0)),) * 2,
        out_shape=(part, part),
        compiler_params=LIMIT,
        name="leaf_partial",
    )(place, in_hbm(leaves))


def leaf_base_kernel(leaf_ref, first_ref, second_ref, out_ref):
    for leaf, ref in enumerate((first_ref, second_ref)):
        inverse = split(ref[...])
        out_ref[leaf] = product(split(leaf_ref[leaf]), inverse, ((1,), (1,)))


def leaf_bases_of(leaves, first, second):
    count, rows, n = leaves.shape
    step = min(rows, 256)
    return pl.pallas_call(
        leaf_base_kernel,
        grid=(rows // step,),
        in_specs=[pl.BlockSpec((count, step, n), lambda g: (0, g, 0))]
        + [pl.BlockSpec((n, n), lambda g: (0, 0))] * 2,
        out_specs=pl.BlockSpec((count, step, n), lambda g: (0, g, 0)),
        out_shape=floats(count, rows, n),
        compiler_params=LIMIT,
        name="leaf_bases",
    )(in_hbm(leaves), first, second)


def factor_kernel(scale, place_ref, own_ref, other_ref, u_ref, v_ref, w_ref):
    n = u_ref.shape[0]
    half, quarter = n // 2, n // 4
    own, other = own_ref[...] * scale, other_ref[...] * scale
    mine = place_ref[0] == 0
    w_ref[:, :n] = jnp.zeros((n, n), jnp.float32)
    for core, part in ((0, jnp.where(mine, own, other)), (1, jnp.where(mine, other, own))):
        square, row, corner = part[:quarter], part[quarter:half], part[half:]
        corner = jnp.concatenate([corner[:, :quarter], corner[:, quarter:]], axis=0)
        start = core * half
        w_ref[start : start + quarter, start : start + half] = square
        w_ref[core * quarter : (core + 1) * quarter, half:n] = row
        start = n - quarter if core == 0 else quarter
        w_ref[start : start + quarter, start : start + quarter] = corner
    ri = lax.broadcasted_iota(jnp.int32, (n, n), 0)
    ci = lax.broadcasted_iota(jnp.int32, (n, n), 1)
    w_ref[:, n:] = jnp.where(ri == ci, 1.0, 0.0)
    full=(SUB,LANE)
    sub=lax.broadcasted_iota(jnp.int32,full,0)
    lane=lax.broadcasted_iota(jnp.int32,full,1)
    zero=jnp.zeros(full,jnp.float32)
    def span(k): return (k//LANE)*LANE, n+((k+SUB+LANE-1)//LANE)*LANE
    def lanebc(x,o): return jnp.broadcast_to(x[:,o:o+1],full)
    def subbc(x,i): return jnp.broadcast_to(x[i:i+1,:],full)
    def load(k):
        lo,hi=span(k)
        P={t: w_ref[k:k+SUB,t*LANE:(t+1)*LANE] for t in range(lo//LANE,hi//LANE)}
        diag={}
        for j in range(SUB):
            c=lanebc(P[lo//LANE],k-lo+j)
            for i in range(j+1): diag[i,j]=subbc(c,i)
        return P,diag
    def loadp(k):
        lo,hi=span(k)
        return {t: w_ref[k:k+SUB,t*LANE:(t+1)*LANE] for t in range(lo//LANE,hi//LANE)}
    def diagof(P,k):
        diag={}
        for j in range(SUB):
            c=lanebc(P[k//LANE],k%LANE+j)
            for i in range(j+1): diag[i,j]=subbc(c,i)
        return diag
    def split3(x):
        h=x.astype(jnp.bfloat16); x=x-h.astype(jnp.float32)
        m=x.astype(jnp.bfloat16); x=x-m.astype(jnp.float32)
        return h,m,x.astype(jnp.bfloat16)
    coming={k: loadp(k) for k in range(0,min(DEPTH*SUB,n),SUB)}
    diag=diagof(coming[0],0)
    for k in range(0,n,SUB):
        lo,hi=span(k)
        tiles=range(lo//LANE,hi//LANE)
        nxt=k+SUB
        P=coming.pop(k)
        if nxt<n: ndiag=diagof(coming[nxt],nxt) if DEPTH>1 else None
        roots=zero
        for i in range(SUB):
            r=lax.rsqrt(diag[i,i])
            roots=jnp.where(sub==i,r,roots)
            if i<SUB-1:
                col=zero
                for j in range(i+1,SUB): col=jnp.where(sub==j,diag[i,j],col)
                col=col*(r*r)
                s={j: diag[i,j]*r for j in range(i+1,SUB)}
                for j in range(i+1,SUB):
                    for l in range(j,SUB): diag[j,l]=diag[j,l]-s[j]*s[l]
                for t in tiles: P[t]=P[t]-col*subbc(P[t],i)
        t0=lo//LANE
        done={t: P[t]*roots for t in tiles}
        done[t0]=jnp.where(lane>=(k-lo)+sub,done[t0],0.0)
        far=k+DEPTH*SUB
        if far<n: coming[far]=loadp(far)
        if nxt<n:
            tn,on=nxt//LANE,nxt%LANE
            E=[lanebc(done[tn],on+j) for j in range(SUB)]
            for i in range(SUB):
                for j in range(i,SUB):
                    ndiag[i,j]=ndiag[i,j]-jnp.broadcast_to(jnp.sum(E[i]*E[j],axis=0,keepdims=True),full)
            for kk in range(SUB):
                row={t: subbc(done[t],kk) for t in done}
                for q in coming:
                    tq,oq=q//LANE,q%LANE
                    c=jnp.sum(jnp.where(lane==oq+sub,row[tq],0.0),axis=1,keepdims=True)
                    c=jnp.broadcast_to(c,full)
                    for t in row:
                        if t in coming[q]: coming[q][t]=coming[q][t]-c*row[t]
        U=jnp.concatenate([done[t] for t in tiles],axis=1)
        if lo: u_ref[k:k+SUB,:lo]=jnp.zeros((SUB,lo),jnp.float32)
        u_ref[k:k+SUB,lo:]=U[:,:n-lo]
        v_ref[k:k+SUB,:hi-n]=U[:,n-lo:]
        if hi<2*n: v_ref[k:k+SUB,hi-n:]=jnp.zeros((SUB,2*n-hi),jnp.float32)
        below=far+SUB
        if below<n:
            lane1=(below//LANE)*LANE
            h,m,l=split3(U[:,lane1-lo:])
            lhs=jnp.concatenate([x[:,:n-lane1].astype(jnp.float32) for x in (h,h,m,h,l,m)],axis=0).astype(jnp.bfloat16)
            rhs=jnp.concatenate([x.astype(jnp.float32) for x in (h,m,h,l,h,m)],axis=0).astype(jnp.bfloat16)
            M=lax.dot_general(lhs,rhs,(((0,),(0,)),((),())),preferred_element_type=jnp.float32)
            w_ref[below:, lane1:hi]=w_ref[below:, lane1:hi]-M[below-lane1:,:]
        if nxt<n: diag=ndiag


def factored(place, own, other, scale):
    n = own.shape[-1] * 2
    return pl.pallas_call(
        functools.partial(factor_kernel, scale),
        in_specs=[SCALARS, WHOLE, WHOLE],
        out_specs=(WHOLE, WHOLE),
        out_shape=(floats(n, n), floats(n, n)),
        scratch_shapes=[pltpu.VMEM((n, 2 * n), jnp.float32)],
        compiler_params=LIMIT,
        name="factor",
    )(place, own, other)


def terms_kernel(*refs):
    count = len(refs) // 3
    for which in range(count):
        high, low = split(refs[which][...])
        refs[count + 2 * which][...] = high
        refs[count + 2 * which + 1][...] = low


def terms_of(slabs, part=0, parts=1):
    depth, n, _ = slabs[0].shape
    depth = depth // parts
    step = 2 if depth % 2 == 0 else 1
    first = part * depth // step
    block = pl.BlockSpec((step, n, n), lambda g: (g, 0, 0))
    outs = pl.pallas_call(
        terms_kernel,
        grid=(depth // step,),
        in_specs=[pl.BlockSpec((step, n, n), lambda g: (first + g, 0, 0))] * len(slabs),
        out_specs=[block] * (2 * len(slabs)),
        out_shape=[jax.ShapeDtypeStruct((depth, n, n), jnp.bfloat16)] * (2 * len(slabs)),
        compiler_params=LIMIT,
        name="terms",
    )(*slabs)
    return [tuple(outs[2 * which : 2 * which + 2]) for which in range(len(slabs))]


def turn_kernel(factor_ref, *refs):
    factor = split(factor_ref[...])
    out_ref = refs[-1]
    for which in range(len(refs) // 2):
        high_ref, low_ref = refs[2 * which : 2 * which + 2]
        for a in range(high_ref.shape[0]):
            turned = product(factor, (high_ref[a], low_ref[a]), ((1,), (0,)))
            out_ref[:, which, a] = turned.reshape(
                out_ref.shape[0], out_ref.shape[3], out_ref.shape[4]
            )


def turned_by(factor, slabs, dests):
    depth, n, _ = slabs[0][0].shape
    cols = factor.shape[0] // dests
    if cols % SUB:
        wide = [high.astype(jnp.float32) + low.astype(jnp.float32) for high, low in slabs]
        rows = factor.reshape(dests, cols, n)
        return jnp.einsum("djb,sabk->dsajk", rows, jnp.stack(wide), precision=FAST)
    step = max(1, 4 // len(slabs))
    step = step if depth % step == 0 else 1
    return pl.pallas_call(
        turn_kernel,
        grid=(depth // step,),
        in_specs=[pl.BlockSpec(factor.shape, lambda g: (0, 0))]
        + [pl.BlockSpec((step, n, n), lambda g: (g, 0, 0))] * (2 * len(slabs)),
        out_specs=pl.BlockSpec((dests, len(slabs), step, cols, n), lambda g: (0, 0, g, 0, 0)),
        out_shape=pltpu.HBM((dests, len(slabs), depth, cols, n), jnp.float32),
        compiler_params=LIMIT,
        name="turn",
    )(factor, *[term for slab in slabs for term in slab])


def move_kernel(place_ref, factor_ref, x_ref, y_ref, *refs):
    moved_refs, (kept_ref, sent_ref, terms_ref) = refs[:-3], refs[-3:]
    step = pl.program_id(0)

    @pl.when(step == 0)
    def _():
        terms_ref[...] = jnp.zeros_like(terms_ref)

    factor = split(factor_ref[...])
    depth, cols, lanes = x_ref.shape
    flat = [ref.reshape(depth * cols, lanes) for ref in (x_ref, y_ref)]
    terms = terms_ref[...]
    for s in range(cols):
        parts = [ref[pl.ds(s, depth, stride=cols), :] for ref in flat]
        moved = product(factor, split(jnp.concatenate(parts, axis=1)), ((1,), (0,)))
        rows = depth // len(moved_refs)
        for which, ref in enumerate(moved_refs):
            ref[s] = moved[which * rows : (which + 1) * rows]
        terms = terms + gram_terms(moved)
    terms_ref[...] = terms

    @pl.when(step == pl.num_programs(0) - 1)
    def _():
        put_parts(gram_of(terms), place_ref[0], kept_ref, sent_ref)


def moved_by(place, factor, gathered, outputs):
    depth, cols, n = gathered.shape
    part = packed_shape(n)
    if cols % SUB:
        moved = jnp.einsum("ia,ajk->jik", factor, gathered, precision=FAST)
        flat = moved.reshape(-1, n)
        gram = jnp.einsum("rc,rd->cd", flat, flat, precision=lax.Precision.HIGHEST)
        parts = packed(gram, 0), packed(gram, 1)
        first = place[0] == 0
        kept, sent = jnp.where(first, *parts), jnp.where(first, *parts[::-1])
        return (*jnp.split(moved, outputs, axis=1), kept, sent)
    rows = depth // outputs
    return pl.pallas_call(
        move_kernel,
        grid=(cols // SUB,),
        in_specs=[
            SCALARS,
            pl.BlockSpec(factor.shape, lambda g: (0, 0)),
            pl.BlockSpec((depth, SUB, n // 2), lambda g: (0, g, 0)),
            pl.BlockSpec((depth, SUB, n // 2), lambda g: (0, g, 1)),
        ],
        out_specs=[pl.BlockSpec((SUB, rows, n), lambda g: (g, 0, 0))] * outputs
        + [pl.BlockSpec(part.shape, lambda g: (0, 0))] * 2,
        out_shape=[floats(cols, rows, n)] * (outputs - 1)
        + [pltpu.HBM((cols, rows, n), jnp.float32), part, part],
        scratch_shapes=[pltpu.VMEM((n, 2 * n), jnp.float32)],
        compiler_params=LIMIT,
        name="move",
    )(place, factor, gathered, gathered)


def base_kernel(inverse_ref, moved_ref, out_ref):
    inverse = split(inverse_ref[...])
    cols, rows, _ = moved_ref.shape
    flat = out_ref.reshape(rows * cols, out_ref.shape[2])
    for s in range(cols):
        flat[pl.ds(s, rows, stride=cols), :] = product(split(moved_ref[s]), inverse, ((1,), (1,)))


def bases_of(inverse, moved):
    cols, rows, n = moved.shape
    if cols % SUB:
        return jnp.einsum("jik,lk->ijl", moved, inverse, precision=FAST)
    return pl.pallas_call(
        base_kernel,
        grid=(cols // SUB, 2),
        in_specs=[
            pl.BlockSpec((n // 2, n), lambda g, h: (h, 0)),
            pl.BlockSpec((SUB, rows, n), lambda g, h: (g, 0, 0)),
        ],
        out_specs=pl.BlockSpec((rows, SUB, n // 2), lambda g, h: (0, g, h)),
        out_shape=floats(rows, cols, n),
        compiler_params=LIMIT,
        name="bases",
    )(inverse, moved)


def joined_kernel(node_ref, inverse_ref, mine_ref, other_ref, out_ref):
    inverse = split(inverse_ref[...])
    cols, rows, _ = mine_ref.shape
    flat = out_ref.reshape(rows * cols, out_ref.shape[2])
    own = pl.program_id(0) == node_ref[0]
    for s in range(cols):
        moved = jnp.where(own, mine_ref[s], other_ref[s])
        flat[pl.ds(s, rows, stride=cols), :] = product(split(moved), inverse, ((1,), (1,)))


def joined_bases(node, inverse, mine, other):
    cols, rows, n = mine.shape
    if cols % SUB:
        left = node[0] == 0
        first, second = jnp.where(left, mine, other), jnp.where(left, other, mine)
        return bases_of(inverse, jnp.concatenate([first, second]))
    return pl.pallas_call(
        joined_kernel,
        grid=(2, 2),
        in_specs=[SCALARS, pl.BlockSpec((n // 2, n), lambda g, h: (h, 0))]
        + [pl.BlockSpec((cols, rows, n), lambda g, h: (0, 0, 0))] * 2,
        out_specs=pl.BlockSpec((rows, cols, n // 2), lambda g, h: (0, g, h)),
        out_shape=floats(rows, 2 * cols, n),
        compiler_params=LIMIT,
        name="joined_bases",
    )(node, inverse, mine, other)


def masks_of():
    masks = [1]
    while 2 * masks[-1] < lax.axis_size("row"):
        masks.append(2 * masks[-1])
    return masks


def first_round(kept, sent):
    return kept + swapped(sent, "row", 1)


def later_rounds(total):
    for mask in masks_of()[1:]:
        total = total + swapped(total, "row", mask)
    return total


def tied(one, other):
    return lax.optimization_barrier((one, other))


def sorted_by(factor, rows_from, cols_from):
    n = factor.shape[0]
    ids = jnp.arange(n, dtype=jnp.int32)
    high = lax.Precision.HIGHEST
    chosen = (ids[:, None] == cols_from[None, :]).astype(jnp.float32)
    factor = jnp.dot(factor, chosen, precision=high)
    chosen = (rows_from[:, None] == ids[None, :]).astype(jnp.float32)
    return jnp.dot(chosen, factor, precision=high)


def body(leaves, level_one, level_two):
    rows = lax.axis_size("row")
    rank = leaves.shape[-1]
    node = lax.axis_index("node") % 2
    is_left = node == 0
    place = jnp.stack([lax.axis_index("row") % 2]).astype(jnp.int32)

    def factors_of(part, scale):
        return factored(place, part, swapped(part, "row", 1), scale)

    own_two = level_two[0]
    sibling_two = swapped(own_two, "node", 1)

    leaf_scale = 1.0 / (leaves.shape[1] * rows)
    masks = masks_of()
    right_part = first_round(*leaf_partial(place, leaves, 1))
    left_part, left_sent = leaf_partial(place, leaves, 0)
    rounds = [lambda part: part + swapped(left_sent, "row", 1)]
    for mask in masks[2:] + masks[1:2]:
        rounds.append(lambda part, mask=mask: part + swapped(part, "row", mask))
    slab = in_hbm(level_one[0])
    slabs = []
    for index, mask in enumerate(masks[1:], 1):
        late = index - len(masks) + 2
        if late >= 0:
            slab, right_part, left_part, slabs = lax.optimization_barrier(
                (slab, right_part, left_part, slabs)
            )
            left_part = rounds[late](left_part)
            slabs = slabs + terms_of([in_hbm(slab)], late, 2)
        right_part = right_part + swapped(right_part, "row", mask)
    right_part, left_part, slabs = lax.optimization_barrier((right_part, left_part, slabs))
    right_upper, right_inverse = factors_of(right_part, leaf_scale)
    right_upper, left_part = tied(right_upper, left_part)
    for later in rounds[2:-1]:
        left_part = later(left_part)
    turned = turned_by(right_upper, slabs, rows)
    turned, left_part = tied(turned, left_part)
    gathered = lax.all_to_all(turned, "row", 0, 0, tiled=True)
    left_part = rounds[-1](left_part)

    left_upper, left_inverse = factors_of(left_part, leaf_scale)
    leaf_bases = leaf_bases_of(leaves, left_inverse, right_inverse)
    gathered, leaf_bases, sibling_two = lax.optimization_barrier(
        (gathered, leaf_bases, sibling_two)
    )

    cols = gathered.shape[3]
    moved_one, kept, sent = moved_by(place, left_upper, gathered.reshape(rank, cols, rank), 1)
    own_part = first_round(kept, sent)
    raw_slabs = [own_two, sibling_two]
    slabs = []
    for index, mask in enumerate(masks[1:], 1):
        late = index - len(masks) + 2
        if late >= 0:
            raw, own_part, slabs = lax.optimization_barrier((raw_slabs[late], own_part, slabs))
            slabs = slabs + terms_of([raw])
        own_part = own_part + swapped(own_part, "row", mask)
    own_part, slabs = tied(own_part, slabs)
    sibling_part = swapped(own_part, "node", 1)
    scale = 1.0 / (rank * rank)
    right_upper, right_inverse = factors_of(jnp.where(is_left, sibling_part, own_part), scale)

    chosen = right_upper.reshape(rows, 2, -1, rank).transpose(1, 0, 2, 3)
    chosen = lax.dynamic_index_in_dim(chosen, node, 0, keepdims=False).reshape(-1, rank)
    turned = turned_by(chosen, slabs, rows)
    gathered = lax.all_to_all(turned, "row", 0, 0, tiled=True)

    left_upper, left_inverse = factors_of(jnp.where(is_left, own_part, sibling_part), scale)
    one_inverse = jnp.where(is_left, left_inverse, right_inverse)
    level_one_bases = bases_of(one_inverse, moved_one)[None]
    ids = jnp.arange(rank, dtype=jnp.int32)
    depth = own_two.shape[0]
    rows_from = 2 * (ids % (rank // 2)) + (ids // (rank // 2) + node) % 2
    cols_from = ids // (2 * depth) * (2 * depth) + 2 * (ids % depth) + (ids // depth + node) % 2
    sorted_left = sorted_by(left_upper, rows_from, cols_from)
    gathered, level_one_bases, sorted_left = lax.optimization_barrier(
        (gathered, level_one_bases, sorted_left)
    )

    cols = gathered.shape[3]
    mine, theirs, kept, sent = moved_by(place, sorted_left, gathered.reshape(rank, cols, rank), 2)
    part = first_round(kept, sent)
    part = part + swapped(part, "node", 1)
    theirs, part = tied(theirs, part)
    received = swapped(theirs, "node", 1)
    two_upper, two_inverse = factors_of(later_rounds(part), scale)
    place = jnp.stack([node]).astype(jnp.int32)
    level_two_bases = joined_bases(place, two_inverse, mine, received)[None]
    return (leaf_bases, level_one_bases, level_two_bases, two_upper[None])


def solution(mesh):
    placed = (P("node", "row", None), P("node", "row", None, None), P("node", "row", None, None))
    return jax.shard_map(
        body,
        mesh=mesh,
        in_specs=placed,
        out_specs=(
            P("node", "row", None),
            P("node", None, "row", None),
            P("node", None, "row", None),
            P("node", None, None),
        ),
        check_vma=False,
    )
```
